128 devices in a mesh: ctx: 16 (over x_lo, y, core), fsdp: 8 (over z, x_hi).
Axes of the slice: x: 4 (x_hi: 2, x_lo: 2; x = x_hi * 2 + x_lo), y: 4, z: 4, core: 2. Of those that a mesh axis runs over, the one named last changes fastest.
Arguments:
- query_rows: bfloat16 [16384, 2048], P('ctx', 'fsdp'), may hold values from -270 to 270
- key_rows: bfloat16 [16384, 1024], P('ctx', 'fsdp'), may hold values from -6 to 6
- value_rows: bfloat16 [16384, 1024], P('ctx', 'fsdp'), may hold values from -6 to 6
- doc_ids: int32 [16384], P('ctx'), may hold values from 0 to 3, never falling along the last dimension, each value on 1 to 6144 neighbouring positions
- out_weight: bfloat16 [2048, 4608], P('fsdp', 'ctx'), may hold values from -0.125 to 0.125
- out_grad: bfloat16 [16384, 4608], P('ctx'), may hold values from -6 to 6
Outputs:
- layer_out: bfloat16 [16384, 4608], P('ctx', 'fsdp')
- query_grad: bfloat16 [16384, 2048], P('ctx', 'fsdp')
- key_grad: bfloat16 [16384, 1024], P('ctx', 'fsdp')
- value_grad: bfloat16 [16384, 1024], P('ctx', 'fsdp')
- weight_grad: float32 [2048, 4608], P('fsdp', 'ctx')
The draws below stay inside these ranges and needn't reach their ends.
Inputs may be any that keep to these rules, and one draw needn't show every extreme that they name: `doc_ids`: never falls along the sequence; each document has 1 to 6144 tokens and one has exactly 6144.
All inputs are finite; a program needn't handle non-finite values.
Results may differ from the reference program's by a relative error of at most 0.035.
Values may be sent and summed in bfloat16 or wider, within the bound.
No kernel may reach another device: no remote copies, remote signals or barrier semaphores. Data moves between devices by JAX's collectives and lax.ppermute only.
A program may use at most 256 MiB of HBM per device.

```python
import math
import jax
import jax.numpy as jnp
import numpy as np
from jax import lax

D = 4608
HEADS = 16
KV_HEADS = 8
HEAD_DIM = 128
WINDOW = 4096
TOK_DEV = 1024
TOKENS = 16384
MOST_DOC = 6144
DOCS = 4
N_CTX = 16
N_FSDP = 8


def shared_keys(key):
    base = jax.random.truncated_normal(jax.random.fold_in(key, 11), -6.0, 6.0, (TOKENS, KV_HEADS * HEAD_DIM), jnp.float32)
    return base


def draw_key_rows(key, part):
    return shared_keys(key).astype(jnp.bfloat16)


def draw_query_rows(key, part):
    drawn = jax.random.truncated_normal(jax.random.fold_in(key, 21), -6.0, 6.0, (TOKENS, HEADS * HEAD_DIM), jnp.float32)
    return drawn.astype(jnp.bfloat16)


def strengthened(result, rng, source, target, blocks, factor):
    def block_of(dim):
        return (jnp.arange(result.shape[dim]) // (result.shape[dim] // blocks)).reshape((-1,) + (1,) * (result.ndim - 1 - dim))

    first = jax.random.permutation(rng, blocks)[block_of(target)]
    far = (block_of(target) + blocks // 2) % blocks
    return jnp.where((block_of(source) == first) | (block_of(source) == far), factor * result, result)


def levels(rng, extent, shards, low, top_value):
    def one(dim, parts):
        heights = jax.random.uniform(jax.random.fold_in(jax.random.fold_in(rng, 6), dim), (parts,), jnp.float32, low / len(shards), top_value / len(shards))
        return jnp.repeat(jnp.exp(heights), extent[dim] // parts).reshape((-1,) + (1,) * (len(extent) - dim - 1))

    gain = one(*shards[0])
    for cut in shards[1:]:
        gain = gain * one(*cut)
    return gain


def profile(count, total, limit, skew):
    weights = [(1 << 20) // math.isqrt(grade ** skew) + 1 for grade in range(2, count + 1)]
    spare, counts = total - limit - (count - 1), [1] * (count - 1)
    while spare > 0:
        free = [i for i in range(count - 1) if counts[i] < limit]
        mass, left = sum([weights[i] for i in free]), spare
        for i in free:
            more = min(limit - counts[i], max(1, left * weights[i] // mass), spare)
            counts[i] = counts[i] + more
            spare = spare - more
    return np.array([limit] + counts)


def ragged(own_key, count, total, bound, slope):
    if count == 2:
        one = jax.random.randint(own_key, (), max(1, total - bound), min(bound, total - 1) + 1)
        return jnp.stack([one, total - one])
    sizes = jnp.asarray(profile(count, total, bound, slope), jnp.int32)
    pairs = (count - 1) // 2
    source_of, receiver = sizes[1:1 + 2 * pairs:2], sizes[2:2 + 2 * pairs:2]
    slack = jnp.minimum(source_of - 1, bound - receiver)
    shifted = jax.random.randint(jax.random.fold_in(own_key, 1), (pairs,), 0, 1 << 20) % (slack + 1)
    sizes = sizes.at[1:1 + 2 * pairs:2].set(source_of - shifted).at[2:2 + 2 * pairs:2].set(receiver + shifted)
    return sizes[jax.random.permutation(jax.random.fold_in(own_key, 2), count)]


def scatter_about(rng, dims, scale, bound, cuts=(), held_as=jnp.bfloat16):
    entries = jax.random.normal(rng, dims, jnp.float32) * scale
    if len(cuts) > 0:
        entries = levels(rng, dims, cuts, -0.22, 0.18) * entries
    return jnp.clip(entries, min=-bound, max=bound).astype(held_as)


def gaussian_with(stream_key, shape, scale, most, pieces, heavy, kind=jnp.bfloat16):
    drawn = scale * jax.random.normal(stream_key, shape, jnp.float32)
    if pieces:
        drawn = drawn * levels(stream_key, shape, pieces, -0.22, 0.18)
    return jnp.clip(strengthened(drawn, jax.random.fold_in(stream_key, 3), *heavy), -most, most).astype(kind)


def setup_inputs(seed: int = 0) -> dict:
    arg_keys = jax.random.split(jax.random.key(seed), 7)
    query_rows = draw_query_rows(jax.random.fold_in(arg_keys[6], 71), 0)
    key_rows = draw_key_rows(jax.random.fold_in(arg_keys[6], 71), 0)
    value_rows = scatter_about(arg_keys[2], (TOKENS, KV_HEADS * HEAD_DIM), 1.0, 6.0, ((0, 16), (1, 8)))
    doc_ids = jnp.searchsorted(jnp.cumsum(ragged(arg_keys[3], DOCS, TOKENS, MOST_DOC, 1)), jnp.arange(TOKENS), side="right").astype(jnp.int32)
    out_weight = scatter_about(arg_keys[4], (HEADS * HEAD_DIM, D), (HEADS * HEAD_DIM) ** -0.5, 0.125, ((0, 8), (1, 16)))
    out_grad = gaussian_with(arg_keys[5], (TOKENS, D), 1.0, 6.0, ((0, 16),), (0, 1, 16, 2.0))
    return {"query_rows": query_rows, "key_rows": key_rows, "value_rows": value_rows, "doc_ids": doc_ids, "out_weight": out_weight, "out_grad": out_grad}


score_scale = 1.0 / 12.0


def reference(query_rows, key_rows, value_rows, doc_ids, out_weight, out_grad):
    reach_count = (WINDOW + TOK_DEV - 1) // TOK_DEV
    span = (reach_count + 1) * TOK_DEV
    front = reach_count * TOK_DEV
    group_size = HEADS // KV_HEADS
    heads_dev = HEADS // N_FSDP
    kv_width = KV_HEADS * HEAD_DIM
    key_pad = jnp.concatenate([jnp.zeros((front, kv_width), key_rows.dtype), key_rows], 0)
    value_pad = jnp.concatenate([jnp.zeros((front, kv_width), value_rows.dtype), value_rows], 0)
    doc_pad = jnp.concatenate([jnp.full((front,), -1, jnp.int32), doc_ids.astype(jnp.int32)], 0)
    distance = jnp.arange(TOK_DEV, dtype=jnp.int32)[:, None] + front - jnp.arange(span, dtype=jnp.int32)[None, :]
    weight_groups = out_weight.reshape(N_FSDP, heads_dev * HEAD_DIM, D).astype(jnp.float32)

    def block(carry, block_index):
        key_acc, value_acc, weight_acc = carry
        first = (block_index * TOK_DEV).astype(jnp.int32)
        query_blk = lax.dynamic_slice_in_dim(query_rows, first, TOK_DEV, 0)
        query_heads = query_blk.reshape(TOK_DEV, KV_HEADS, group_size, HEAD_DIM).astype(jnp.float32)
        key_heads = lax.dynamic_slice_in_dim(key_pad, first, span, 0).reshape(span, KV_HEADS, HEAD_DIM).astype(jnp.float32)
        value_heads = lax.dynamic_slice_in_dim(value_pad, first, span, 0).reshape(span, KV_HEADS, HEAD_DIM).astype(jnp.float32)
        doc_query = lax.dynamic_slice_in_dim(doc_ids.astype(jnp.int32), first, TOK_DEV, 0)
        doc_key = lax.dynamic_slice_in_dim(doc_pad, first, span, 0)
        visible = (doc_query[:, None] == doc_key[None, :]) & (distance >= 0) & (distance < WINDOW)
        scores = jnp.einsum("ikgd,jkd->kgij", query_heads, key_heads) * score_scale
        scores = jnp.where(visible[None, None], scores, -jnp.inf)
        row_max = jnp.max(scores, axis=-1, keepdims=True)
        expo = jnp.exp(scores - row_max)
        probs = expo / jnp.sum(expo, axis=-1, keepdims=True)
        probs_b = probs.astype(jnp.bfloat16)
        attn_heads = jnp.einsum("kgij,jkd->ikgd", probs_b.astype(jnp.float32), value_heads).astype(jnp.bfloat16)
        attn_flat = attn_heads.reshape(TOK_DEV, HEADS * HEAD_DIM)
        attn_groups = attn_flat.reshape(TOK_DEV, N_FSDP, heads_dev * HEAD_DIM).astype(jnp.float32)
        partials = jnp.einsum("ifc,fcd->fid", attn_groups, weight_groups).astype(jnp.bfloat16)
        partials = lax.optimization_barrier(partials).astype(jnp.float32)
        out_blk = jnp.sum(partials, axis=0).astype(jnp.bfloat16)
        grad_blk = lax.dynamic_slice_in_dim(out_grad, first, TOK_DEV, 0)
        d_attn = jnp.dot(grad_blk, out_weight.T, preferred_element_type=jnp.float32).astype(jnp.bfloat16)
        weight_acc = weight_acc + jnp.dot(attn_flat.T, grad_blk, preferred_element_type=jnp.float32)
        d_heads = d_attn.reshape(TOK_DEV, KV_HEADS, group_size, HEAD_DIM).astype(jnp.float32)
        delta = jnp.einsum("ikgd,ikgd->kgi", d_heads, attn_heads.astype(jnp.float32))
        d_probs = jnp.einsum("ikgd,jkd->kgij", d_heads, value_heads)
        d_scores = (probs * (d_probs - delta[..., None])).astype(jnp.bfloat16).astype(jnp.float32)
        query_grad = (score_scale * jnp.einsum("kgij,jkd->ikgd", d_scores, key_heads)).astype(jnp.bfloat16)
        key_part = score_scale * jnp.einsum("kgij,ikgd->jkd", d_scores, query_heads)
        value_part = jnp.einsum("kgij,ikgd->jkd", probs_b.astype(jnp.float32), d_heads)
        key_old = lax.dynamic_slice_in_dim(key_acc, first, span, 0)
        value_old = lax.dynamic_slice_in_dim(value_acc, first, span, 0)
        key_acc = lax.dynamic_update_slice_in_dim(key_acc, key_old + key_part.reshape(span, kv_width), first, 0)
        value_acc = lax.dynamic_update_slice_in_dim(value_acc, value_old + value_part.reshape(span, kv_width), first, 0)
        return (key_acc, value_acc, weight_acc), (out_blk, query_grad.reshape(TOK_DEV, HEADS * HEAD_DIM))

    start_carry = (jnp.zeros((front + TOKENS, kv_width), jnp.float32), jnp.zeros((front + TOKENS, kv_width), jnp.float32), jnp.zeros((HEADS * HEAD_DIM, D), jnp.float32))
    final, stacked = lax.scan(block, start_carry, jnp.arange(N_CTX, dtype=jnp.int32))
    key_acc, value_acc, weight_grad = final
    layer_out = stacked[0].reshape(TOKENS, D)
    query_grad = stacked[1].reshape(TOKENS, HEADS * HEAD_DIM)
    key_grad = key_acc[front:].astype(jnp.bfloat16)
    value_grad = value_acc[front:].astype(jnp.bfloat16)
    return (layer_out, query_grad, key_grad, value_grad, weight_grad)
```

```python
import functools
import math

import jax
import jax.numpy as jnp
from jax import lax
from jax.experimental import pallas as pl
from jax.experimental.pallas import tpu as pltpu
from jax.sharding import Mesh, PartitionSpec as P

HEAD_DIM = 128
WINDOW = 4096
N_DOCS = 4
SCALE = 1.0 / 12.0
SCALE2 = math.log2(math.e) / 12.0
NEG = -1e30
FAR = 1 << 30
F32 = jnp.float32
BF16 = jnp.bfloat16
NT = (((1,), (1,)), ((), ()))
NN = (((1,), (0,)), ((), ()))

CTX = ("xl", "y", "core")
FSDP = ("z", "xh")


def first_seen(meta, i):
    low = i + 1
    for d in range(N_DOCS):
        low = jnp.maximum(low, jnp.where(i >= meta[d], meta[N_DOCS + d], 0))
    return low


def tile_bounds(meta, q0, bq, bk, win):
    start = first_seen(meta, q0) // bk
    end = (win + q0 + bq - 1) // bk + 1
    b = (win + q0 + 1) // bk
    a = (first_seen(meta, q0 + bq - 1) + bk - 1) // bk
    a = jnp.clip(a, start, end)
    b = jnp.clip(b, a, end)
    return start, a, b, end


def heads_of(ref, q0, bq):
    return jnp.concatenate(
        [ref[q0 : q0 + bq, 0:HEAD_DIM], ref[q0 : q0 + bq, HEAD_DIM : 2 * HEAD_DIM]], 0
    )


def masked_tile(meta, tile, q0, r, win, bq, bk):
    i = q0 + lax.broadcasted_iota(jnp.int32, (1, bq), 1)
    low = first_seen(meta, i) - r
    high = win + i - r
    row = lax.broadcasted_iota(jnp.int32, (bk, bq), 0)
    seen = (row >= low) & (row <= high)
    return jnp.concatenate(
        [jnp.where(seen, tile[:, :bq], NEG), jnp.where(seen, tile[:, bq:], NEG)], 1
    )


def forward_kernel(meta, q_ref, kv_ref, o_ref, lse_ref, m_ref, acc_ref, *, bq, bk):
    tok = q_ref.shape[0]
    win = kv_ref.shape[0] - tok
    for q0 in range(0, tok, bq):
        q2 = heads_of(q_ref, q0, bq)
        m_ref[...] = jnp.full(m_ref.shape, NEG, F32)
        acc_ref[...] = jnp.zeros(acc_ref.shape, F32)
        start, a, b, end = tile_bounds(meta, q0, bq, bk, win)

        def tile(j, masked):
            r = pl.multiple_of(j * bk, bk)
            k = kv_ref[pl.ds(r, bk), 0:HEAD_DIM]
            v = kv_ref[pl.ds(r, bk), HEAD_DIM : 2 * HEAD_DIM]
            s = lax.dot_general(k, q2, NT, preferred_element_type=F32)
            if masked:
                s = masked_tile(meta, s, q0, r, win, bq, bk)
            m_old = m_ref[0:1, :]
            m_new = jnp.maximum(m_old, jnp.max(s, axis=0, keepdims=True))
            p = jnp.exp2((s - m_new) * SCALE2)
            shrink = jnp.exp2((m_old - m_new) * SCALE2)
            v_ones = jnp.concatenate([v.T, jnp.ones((16, bk), BF16)], 0)
            acc_ref[...] = acc_ref[...] * shrink + lax.dot_general(
                v_ones, p.astype(BF16), NN, preferred_element_type=F32
            )
            m_ref[...] = jnp.broadcast_to(m_new, m_ref.shape)

        def down(high, low, masked):
            def step(t, carry):
                tile(high - 1 - t, masked)
                return carry

            lax.fori_loop(0, high - low, step, 0)

        down(end, b, True)
        down(b, a, False)
        down(a, start, True)
        total = acc_ref[HEAD_DIM : HEAD_DIM + 1, :]
        o = (acc_ref[0:HEAD_DIM, :] / total).T
        o_ref[q0 : q0 + bq, 0:HEAD_DIM] = o[:bq].astype(BF16)
        o_ref[q0 : q0 + bq, HEAD_DIM:] = o[bq:].astype(BF16)
        lse = m_ref[...] * SCALE2 + jnp.log2(acc_ref[HEAD_DIM : HEAD_DIM + 8, :])
        lse_ref[0:8, q0 : q0 + bq] = lse[:, :bq]
        lse_ref[8:16, q0 : q0 + bq] = lse[:, bq:]


def forward(meta, q, kv, bq=512, bk=512):
    tok = q.shape[0]
    vmem = pl.BlockSpec(memory_space=pltpu.VMEM)
    return pl.pallas_call(
        functools.partial(forward_kernel, bq=bq, bk=bk),
        out_shape=(
            jax.ShapeDtypeStruct((tok, 2 * HEAD_DIM), BF16),
            jax.ShapeDtypeStruct((16, tok), F32),
        ),
        in_specs=[pl.BlockSpec(memory_space=pltpu.SMEM), vmem, vmem],
        out_specs=(vmem, vmem),
        scratch_shapes=[
            pltpu.VMEM((8, 2 * bq), F32),
            pltpu.VMEM((HEAD_DIM + 16, 2 * bq), F32),
        ],
        compiler_params=pltpu.CompilerParams(vmem_limit_bytes=40 * 2**20),
        cost_estimate=pl.CostEstimate(
            flops=20_000_000_000, bytes_accessed=4_000_000, transcendentals=9_000_000
        ),
        name="attn_forward",
    )(meta, q, kv)


def backward_kernel(
    meta, q_ref, kv_ref, o_ref, do_ref, lse_ref, dq_ref, dkv_ref, own_ref, dqt, dk, dv, *, bq, bk
):
    tok = q_ref.shape[0]
    win = kv_ref.shape[0] - tok
    dk[...] = jnp.zeros(dk.shape, F32)
    dv[...] = jnp.zeros(dv.shape, F32)
    for q0 in range(0, tok, bq):
        q2 = heads_of(q_ref, q0, bq)
        do2 = heads_of(do_ref, q0, bq)
        o2 = heads_of(o_ref, q0, bq)
        delta = jnp.sum((do2.astype(F32) * o2.astype(F32)).T, axis=0, keepdims=True)
        lse = jnp.concatenate([lse_ref[0:1, q0 : q0 + bq], lse_ref[8:9, q0 : q0 + bq]], 1)
        dqt[...] = jnp.zeros(dqt.shape, F32)
        start, a, b, end = tile_bounds(meta, q0, bq, bk, win)

        def tile(j, masked):
            r = pl.multiple_of(j * bk, bk)
            k = kv_ref[pl.ds(r, bk), 0:HEAD_DIM]
            v = kv_ref[pl.ds(r, bk), HEAD_DIM : 2 * HEAD_DIM]
            t = lax.dot_general(k, q2, NT, preferred_element_type=F32) * SCALE2 - lse
            if masked:
                t = masked_tile(meta, t, q0, r, win, bq, bk)
            p = jnp.exp2(t)
            dp = lax.dot_general(v, do2, NT, preferred_element_type=F32)
            ds = (p * (dp - delta)).astype(BF16)
            dv[pl.ds(r, bk), :] += lax.dot_general(
                p.astype(BF16), do2, NN, preferred_element_type=F32
            )
            dk[pl.ds(r, bk), :] += lax.dot_general(ds, q2, NN, preferred_element_type=F32)
            dqt[...] += lax.dot_general(k.T, ds, NN, preferred_element_type=F32)

        def up(low, high, masked):
            def step(t, carry):
                tile(t, masked)
                return carry

            lax.fori_loop(low, high, step, 0)

        up(start, a, True)
        up(a, b, False)
        up(b, end, True)
        dq = (dqt[...] * SCALE).T
        dq_ref[q0 : q0 + bq, 0:HEAD_DIM] = dq[:bq].astype(BF16)
        dq_ref[q0 : q0 + bq, HEAD_DIM:] = dq[bq:].astype(BF16)
    dkv_ref[:, 0:HEAD_DIM] = (dk[0:win] * SCALE).astype(BF16)
    dkv_ref[:, HEAD_DIM:] = dv[0:win].astype(BF16)
    own_ref[:, 0:HEAD_DIM] = dk[win:] * SCALE
    own_ref[:, HEAD_DIM:] = dv[win:]


def backward(meta, q, kv, o, do, lse, bq=512, bk=512):
    tok = q.shape[0]
    win = kv.shape[0] - tok
    vmem = pl.BlockSpec(memory_space=pltpu.VMEM)
    return pl.pallas_call(
        functools.partial(backward_kernel, bq=bq, bk=bk),
        out_shape=(
            jax.ShapeDtypeStruct((tok, 2 * HEAD_DIM), BF16),
            jax.ShapeDtypeStruct((win, 2 * HEAD_DIM), BF16),
            jax.ShapeDtypeStruct((tok, 2 * HEAD_DIM), F32),
        ),
        in_specs=[pl.BlockSpec(memory_space=pltpu.SMEM)] + [vmem] * 5,
        out_specs=(vmem, vmem, vmem),
        scratch_shapes=[
            pltpu.VMEM((HEAD_DIM, 2 * bq), F32),
            pltpu.VMEM((tok + win, HEAD_DIM), F32),
            pltpu.VMEM((tok + win, HEAD_DIM), F32),
        ],
        compiler_params=pltpu.CompilerParams(vmem_limit_bytes=40 * 2**20),
        cost_estimate=pl.CostEstimate(
            flops=30_000_000_000, bytes_accessed=8_000_000, transcendentals=9_000_000
        ),
        name="attn_backward",
    )(meta, q, kv, o, do, lse)


def ctx_shift(value, steps):
    count = lax.axis_size(CTX)
    leading, last = max(0, -steps), min(count, count - steps)
    return lax.ppermute(value, CTX, [(s, s + steps) for s in range(leading, last)])


def swap(value, axis):
    return lax.ppermute(value, axis, [(0, 1), (1, 0)])


def z_shift(value, steps):
    count = lax.axis_size("z")
    return lax.ppermute(value, "z", [(s, (s + steps) % count) for s in range(count)])


def body(query_rows, key_rows, value_rows, doc_ids, out_weight, out_grad):
    tok = query_rows.shape[0]
    core = lax.axis_index("core")
    z = lax.axis_index("z")
    xh = lax.axis_index("xh")
    n_z = lax.axis_size("z")

    docs = lax.iota(jnp.int32, N_DOCS)
    count = jnp.sum((doc_ids[None, :] == docs[:, None]).astype(jnp.int32), axis=1)
    info = jnp.stack([count // 32, count % 32]).astype(BF16)
    info = jnp.pad(info, ((0, 14), (0, 2 * HEAD_DIM - N_DOCS)))
    kv = jnp.concatenate([key_rows, value_rows], 1)
    load = jnp.concatenate([kv, info], 0)
    back2 = ctx_shift(load, 2)
    back4 = ctx_shift(load, 4)
    back1 = swap(jnp.where(core == 0, load, back2), "core")
    back3 = swap(jnp.where(core == 0, back2, back4), "core")
    blocks = [back4, back3, back2, back1]
    window = jnp.concatenate([b[:tok] for b in blocks] + [kv], 0)
    infos = sum(b[tok : tok + 2, :N_DOCS].astype(F32) for b in blocks)
    before = (infos[0] * 32 + infos[1]).astype(jnp.int32)
    local_start = jnp.cumsum(count) - count
    present = count > 0
    meta = jnp.concatenate(
        [
            jnp.where(present, local_start, FAR),
            jnp.where(present, WINDOW + local_start - before, 0),
        ]
    )

    weight_t = lax.all_gather(out_weight.T, CTX, axis=0, tiled=True)
    attn, lse = forward(meta, query_rows, window)
    d_attn = jnp.dot(out_grad, weight_t, preferred_element_type=F32).astype(BF16)

    weight_z = weight_t.reshape(n_z, -1, weight_t.shape[1])

    def weight_for(steps):
        return lax.dynamic_index_in_dim(weight_z, (z + steps) % n_z, 0, keepdims=False)

    weights = [weight_for(0)] + [z_shift(weight_for(s), s) for s in range(1, n_z)]
    attns = [attn] + [z_shift(attn, s) for s in range(1, n_z)]
    cols = weights[0].shape[0] // 2

    def out_part(half):
        total = None
        for a, w in zip(attns, weights):
            w = lax.dynamic_slice_in_dim(w, half * cols, cols, 0)
            term = lax.dot_general(a, w, NT, preferred_element_type=F32)
            total = term if total is None else total + term
        return total

    out_other = swap(out_part(1 - xh).astype(BF16), "xh")

    d_weight = lax.dot_general(
        out_grad, attn, (((0,), (0,)), ((), ())), preferred_element_type=F32
    ).astype(BF16)
    weight_grad = lax.psum_scatter(d_weight, CTX, scatter_dimension=0, tiled=True).astype(F32).T

    query_grad, d_window, own = backward(meta, query_rows, window, attn, d_attn, lse)
    part4, part3, part2, part1 = (d_window[i * tok : (i + 1) * tok] for i in range(4))
    other3 = swap(part3, "core").astype(F32)
    other1 = swap(part1, "core").astype(F32)
    even = core == 0
    sum4 = (part4.astype(F32) + jnp.where(even, 0.0, other3)).astype(BF16)
    sum2 = (part2.astype(F32) + jnp.where(even, other3, other1)).astype(BF16)
    own = own + jnp.where(even, other1, 0.0)
    own = own + ctx_shift(sum4, -4).astype(F32) + ctx_shift(sum2, -2).astype(F32)
    own = own.astype(BF16)

    layer_out = (out_part(xh) + out_other.astype(F32)).astype(BF16)
    return layer_out, query_grad, own[:, :HEAD_DIM], own[:, HEAD_DIM:], weight_grad


def solution(mesh):
    fine = Mesh(mesh.devices.reshape(2, 4, 2, 4, 2), CTX + FSDP)
    in_specs = (
        P(CTX, FSDP),
        P(CTX, FSDP),
        P(CTX, FSDP),
        P(CTX),
        P(FSDP, CTX),
        P(CTX, None),
    )
    out_specs = (
        P(CTX, FSDP),
        P(CTX, FSDP),
        P(CTX, FSDP),
        P(CTX, FSDP),
        P(FSDP, CTX),
    )
    return jax.shard_map(body, mesh=fine, in_specs=in_specs, out_specs=out_specs, check_vma=False)
```

```python
import functools
import math

import jax
import jax.numpy as jnp
from jax import lax
from jax.experimental import pallas as pl
from jax.experimental.pallas import tpu as pltpu
from jax.sharding import Mesh, PartitionSpec as P

HEAD_DIM = 128
WINDOW = 4096
N_DOCS = 4
SCALE = 1.0 / 12.0
SCALE2 = math.log2(math.e) / 12.0
NEG = -1e30
FAR = 1 << 30
F32 = jnp.float32
BF16 = jnp.bfloat16
NT = (((1,), (1,)), ((), ()))
NN = (((1,), (0,)), ((), ()))

TOK = 1024
BQ = 512
BK = 512

CTX = ("xl", "y", "core")
FSDP = ("z", "xh")


def first_seen(meta, i):
    low = i + 1
    for d in range(N_DOCS):
        low = jnp.maximum(low, jnp.where(i >= meta[d], meta[N_DOCS + d], 0))
    return low


def heads_of(ref, q0):
    rows = pl.ds(q0, BQ)
    return jnp.concatenate([ref[rows, 0:HEAD_DIM], ref[rows, HEAD_DIM : 2 * HEAD_DIM]], 0)


def masked_tile(meta, tile, q0, place):
    i = q0 + lax.broadcasted_iota(jnp.int32, (1, BQ), 1)
    low = first_seen(meta, i) - place
    high = WINDOW + i - place
    row = lax.broadcasted_iota(jnp.int32, (BK, BQ), 0)
    seen = (row >= low) & (row <= high)
    return jnp.concatenate(
        [jnp.where(seen, tile[:, :BQ], NEG), jnp.where(seen, tile[:, BQ:], NEG)], 1
    )


def for_tiles(meta, q0, base, rows, tile):
    low_first = first_seen(meta, q0)
    low_last = first_seen(meta, q0 + BQ - 1)
    begin = jnp.maximum(low_first - base, 0) // BK
    end = jnp.minimum((WINDOW + q0 + BQ - 1 - base) // BK + 1, rows // BK)

    def step(t, carry):
        row = pl.multiple_of((end - 1 - t) * BK, BK)
        place = base + row
        plain = (place >= low_last) & (place + BK - 1 <= WINDOW + q0)

        @pl.when(plain)
        def _():
            tile(row, place, False)

        @pl.when(jnp.logical_not(plain))
        def _():
            tile(row, place, True)

        return carry

    lax.fori_loop(0, end - begin, step, 0)


def for_queries(tok, work):
    def step(t, carry):
        work(pl.multiple_of(t * BQ, BQ), pl.multiple_of(t * 2 * BQ, 2 * BQ))
        return carry

    lax.fori_loop(0, tok // BQ, step, 0)


def forward_tile(meta, q2, q0, k_ref, v_ref, m_ref, acc_ref, row, place, masked):
    k = k_ref[pl.ds(row, BK), :]
    v = v_ref[pl.ds(row, BK), :]
    s = lax.dot_general(k, q2, NT, preferred_element_type=F32)
    if masked:
        s = masked_tile(meta, s, q0, place)
    m_old = m_ref[0:1, :]
    m_new = jnp.maximum(m_old, jnp.max(s, axis=0, keepdims=True))
    p = jnp.exp2((s - m_new) * SCALE2)
    shrink = jnp.exp2((m_old - m_new) * SCALE2)
    v_ones = jnp.concatenate([v.T, jnp.ones((16, BK), BF16)], 0)
    acc_ref[...] = acc_ref[...] * shrink + lax.dot_general(
        v_ones, p.astype(BF16), NN, preferred_element_type=F32
    )
    m_ref[...] = jnp.broadcast_to(m_new, m_ref.shape)


def key_part(ref):
    return ref.at[:, 0:HEAD_DIM]


def value_part(ref):
    return ref.at[:, HEAD_DIM : 2 * HEAD_DIM]


def near_kernel(meta, q_ref, kv_ref, two_ref, odd_ref, m_out, acc_out, m_ref, acc_ref):
    tok = q_ref.shape[0]
    blocks = ((kv_ref, WINDOW), (two_ref, WINDOW - 2 * tok), (odd_ref, meta[8]))

    def work(q0, c0):
        q2 = heads_of(q_ref, q0)
        m_ref[...] = jnp.full(m_ref.shape, NEG, F32)
        acc_ref[...] = jnp.zeros(acc_ref.shape, F32)
        for ref, base in blocks:
            tile = functools.partial(
                forward_tile, meta, q2, q0, key_part(ref), value_part(ref), m_ref, acc_ref
            )
            for_tiles(meta, q0, base, tok, tile)
        m_out[:, pl.ds(c0, 2 * BQ)] = m_ref[...]
        acc_out[:, pl.ds(c0, 2 * BQ)] = acc_ref[...]

    for_queries(tok, work)


def far_kernel(meta, q_ref, four_ref, rest_ref, m_in, acc_in, o_ref, lse_ref, m_ref, acc_ref):
    tok = q_ref.shape[0]
    blocks = ((rest_ref, meta[9]), (four_ref, WINDOW - 4 * tok))

    def work(q0, c0):
        q2 = heads_of(q_ref, q0)
        m_ref[...] = m_in[:, pl.ds(c0, 2 * BQ)]
        acc_ref[...] = acc_in[:, pl.ds(c0, 2 * BQ)]
        for ref, base in blocks:
            tile = functools.partial(
                forward_tile, meta, q2, q0, key_part(ref), value_part(ref), m_ref, acc_ref
            )
            for_tiles(meta, q0, base, tok, tile)
        o = (acc_ref[0:HEAD_DIM, :] / acc_ref[HEAD_DIM : HEAD_DIM + 1, :]).T
        o_ref[pl.ds(q0, BQ), 0:HEAD_DIM] = o[:BQ].astype(BF16)
        o_ref[pl.ds(q0, BQ), HEAD_DIM : 2 * HEAD_DIM] = o[BQ:].astype(BF16)
        lse_ref[:, pl.ds(c0, 2 * BQ)] = m_ref[...] * SCALE2 + jnp.log2(
            acc_ref[HEAD_DIM : HEAD_DIM + 8, :]
        )

    for_queries(tok, work)


def call(kernel, name, n_vmem, out_shape, scratch, vmem_mb, cost=0):
    vmem = pl.BlockSpec(memory_space=pltpu.VMEM)
    return pl.pallas_call(
        kernel,
        out_shape=out_shape,
        in_specs=[pl.BlockSpec(memory_space=pltpu.SMEM)] + [vmem] * n_vmem,
        out_specs=jax.tree.map(lambda _: vmem, out_shape),
        scratch_shapes=scratch,
        compiler_params=pltpu.CompilerParams(vmem_limit_bytes=vmem_mb * 2**20),
        cost_estimate=pl.CostEstimate(flops=cost, bytes_accessed=0, transcendentals=0),
        name=name,
    )


def forward_scratch():
    return [pltpu.VMEM((8, 2 * BQ), F32), pltpu.VMEM((HEAD_DIM + 16, 2 * BQ), F32)]


def forward_near(meta, q, kv, two, odd):
    tok = q.shape[0]
    out = (
        jax.ShapeDtypeStruct((8, 2 * tok), F32),
        jax.ShapeDtypeStruct((HEAD_DIM + 16, 2 * tok), F32),
    )
    return call(near_kernel, "attn_near", 4, out, forward_scratch(), 24)(meta, q, kv, two, odd)


def forward_far(meta, q, four, rest, m, acc):
    tok = q.shape[0]
    out = (
        jax.ShapeDtypeStruct((tok, 2 * HEAD_DIM), BF16),
        jax.ShapeDtypeStruct((8, 2 * tok), F32),
    )
    return call(far_kernel, "attn_far", 5, out, forward_scratch(), 24)(meta, q, four, rest, m, acc)


def backward_kernel(bases, first, last, meta, q_ref, do_ref, o_ref, lse_ref, *refs):
    tok = q_ref.shape[0]
    n = len(bases)
    block_refs, refs = refs[:n], refs[n:]
    if not first:
        dqt_in, refs = refs[0], refs[1:]
    part_refs, dq_ref, (dqt, dk, dv) = refs[:n], refs[n], refs[n + 1 :]
    dk[...] = jnp.zeros(dk.shape, F32)
    dv[...] = jnp.zeros(dv.shape, F32)

    def work(q0, c0):
        cols = pl.ds(c0, 2 * BQ)
        q2 = heads_of(q_ref, q0)
        do2 = heads_of(do_ref, q0)
        o2 = heads_of(o_ref, q0)
        delta = jnp.sum((do2.astype(F32) * o2.astype(F32)).T, axis=0, keepdims=True)
        lse = lse_ref[0:1, cols]
        dqt[...] = jnp.zeros(dqt.shape, F32) if first else dqt_in[:, cols]

        def tile(index, row, place, masked):
            ref = block_refs[index]
            k = ref[pl.ds(row, BK), 0:HEAD_DIM]
            v = ref[pl.ds(row, BK), HEAD_DIM : 2 * HEAD_DIM]
            t = lax.dot_general(k, q2, NT, preferred_element_type=F32) * SCALE2 - lse
            if masked:
                t = masked_tile(meta, t, q0, place)
            p = jnp.exp2(t)
            dp = lax.dot_general(v, do2, NT, preferred_element_type=F32)
            ds = (p * (dp - delta)).astype(BF16)
            rows = pl.ds(row, BK)
            dv[index, rows, :] += lax.dot_general(
                p.astype(BF16), do2, NN, preferred_element_type=F32
            )
            dk[index, rows, :] += lax.dot_general(ds, q2, NN, preferred_element_type=F32)
            dqt[...] += lax.dot_general(k.T, ds, NN, preferred_element_type=F32)

        for index, base in enumerate(bases):
            base = base if base >= 0 else meta[-base]
            for_tiles(meta, q0, base, tok, functools.partial(tile, index))
        if last:
            dq = (dqt[...] * SCALE).T
            dq_ref[pl.ds(q0, BQ), 0:HEAD_DIM] = dq[:BQ].astype(BF16)
            dq_ref[pl.ds(q0, BQ), HEAD_DIM : 2 * HEAD_DIM] = dq[BQ:].astype(BF16)
        else:
            dq_ref[:, cols] = dqt[...]

    for_queries(tok, work)
    for index, ref in enumerate(part_refs):
        ref[:, 0:HEAD_DIM] = (dk[index] * SCALE).astype(ref.dtype)
        ref[:, HEAD_DIM : 2 * HEAD_DIM] = dv[index].astype(ref.dtype)


def backward(name, meta, common, blocks, bases, dqt=None, last=False):
    tok = common[0].shape[0]
    n = len(blocks)
    part = jax.ShapeDtypeStruct((tok, 2 * HEAD_DIM), F32 if last else BF16)
    dq = ((tok, 2 * HEAD_DIM), BF16) if last else ((HEAD_DIM, 2 * tok), F32)
    scratch = [
        pltpu.VMEM((HEAD_DIM, 2 * BQ), F32),
        pltpu.VMEM((n, tok, HEAD_DIM), F32),
        pltpu.VMEM((n, tok, HEAD_DIM), F32),
    ]
    args = list(common) + list(blocks) + ([] if dqt is None else [dqt])
    kernel = functools.partial(backward_kernel, bases, dqt is None, last)
    out = (part,) * n + (jax.ShapeDtypeStruct(*dq),)
    return call(kernel, name, len(args), out, scratch, 30)(meta, *args)


def projection_kernel(core, og_ref, wt_ref, attn_ref, d_attn_ref, mine_ref, other_ref, total, attn_t):
    step = pl.program_id(0)
    rows = mine_ref.shape[0] // 2

    @pl.when(step == 0)
    def _():
        total[...] = jnp.zeros(total.shape, F32)
        attn_t[...] = attn_ref[...].T

    og = og_ref[...]
    total[...] += lax.dot_general(og, wt_ref[...], NN, preferred_element_type=F32)
    dw = lax.dot_general(attn_t[...], og, NN, preferred_element_type=F32).T.astype(BF16)
    even = core[0] == 0
    for c in range(2):
        to = pl.ds(c * rows, rows)
        zero = dw[2 * c * rows : (2 * c + 1) * rows]
        one = dw[(2 * c + 1) * rows : (2 * c + 2) * rows]
        mine_ref[to, :] = jnp.where(even, zero, one)
        other_ref[to, :] = jnp.where(even, one, zero)

    @pl.when(step == pl.num_programs(0) - 1)
    def _():
        d_attn_ref[...] = total[...].astype(BF16)


def projection(core, out_grad, weight_t, attn, chunk):
    tok, width = out_grad.shape
    heads = attn.shape[1]
    whole = pl.BlockSpec((tok, heads), lambda i: (0, 0))
    half = pl.BlockSpec((chunk // 2, heads), lambda i: (i, 0))
    return pl.pallas_call(
        projection_kernel,
        grid=(width // chunk,),
        out_shape=(
            jax.ShapeDtypeStruct((tok, heads), BF16),
            jax.ShapeDtypeStruct((width // 2, heads), BF16),
            jax.ShapeDtypeStruct((width // 2, heads), BF16),
        ),
        in_specs=[
            pl.BlockSpec(memory_space=pltpu.SMEM),
            pl.BlockSpec((tok, chunk), lambda i: (0, i)),
            pl.BlockSpec((chunk, heads), lambda i: (i, 0)),
            whole,
        ],
        out_specs=(whole, half, half),
        scratch_shapes=[pltpu.VMEM((tok, heads), F32), pltpu.VMEM((heads, tok), BF16)],
        compiler_params=pltpu.CompilerParams(vmem_limit_bytes=24 * 2**20),
        cost_estimate=pl.CostEstimate(
            flops=1_000_000_000, bytes_accessed=1_000_000, transcendentals=0
        ),
        name="projection",
    )(core, out_grad, weight_t, attn)


def out_kernel(where, attn_ref, *refs):
    n = attn_ref.shape[0] // TOK
    weights, out_ref = refs[:n], refs[-1]
    cols = out_ref.shape[0]
    rows = pl.ds(pl.multiple_of(where[0] * cols, 16), cols)
    total = refs[n][...].astype(F32) if len(refs) == n + 2 else None
    for steps, w in enumerate(weights):
        origin = lax.rem(where[1] + n - steps, n)
        a = attn_ref[pl.ds(pl.multiple_of(origin * TOK, TOK), TOK), :]
        term = lax.dot_general(w[rows, :], a, NT, preferred_element_type=F32)
        total = term if total is None else total + term
    out_ref[...] = total.astype(BF16)


def out_part(name, where, attn_all, weights, extra=()):
    args = [attn_all] + list(weights) + list(extra)
    out = jax.ShapeDtypeStruct((weights[0].shape[0] // 2, TOK), BF16)
    return call(out_kernel, name, len(args), out, [], 24)(where, *args)


def ctx_shift(value, steps):
    count = lax.axis_size(CTX)
    leading, last = max(0, -steps), min(count, count - steps)
    return lax.ppermute(value, CTX, [(s, s + steps) for s in range(leading, last)])


def swap(value, axis):
    return lax.ppermute(value, axis, [(0, 1), (1, 0)])


def z_shift(value, steps):
    count = lax.axis_size("z")
    return lax.ppermute(value, "z", [(s, (s + steps) % count) for s in range(count)])


def body(query_rows, key_rows, value_rows, doc_ids, out_weight, out_grad):
    tok = query_rows.shape[0]
    core = lax.axis_index("core")
    even = core == 0
    z = lax.axis_index("z")
    xh = lax.axis_index("xh")
    n_z = lax.axis_size("z")

    weight_t = lax.all_gather(out_weight.T, CTX, axis=0, tiled=True)

    docs = lax.iota(jnp.int32, N_DOCS)
    count = jnp.sum((doc_ids[None, :] == docs[:, None]).astype(jnp.int32), axis=1)
    info = jnp.stack([count // 32, count % 32]).astype(BF16)
    info = jnp.pad(info, ((0, 14), (0, 2 * HEAD_DIM - N_DOCS)))
    kv = jnp.concatenate([jnp.concatenate([key_rows, value_rows], 1), info], 0)
    two = ctx_shift(kv, 2)
    four = ctx_shift(kv, 4)
    odd = swap(two, "core")

    def count_of(block):
        high, low = block[tok, :N_DOCS], block[tok + 1, :N_DOCS]
        return (high.astype(F32) * 32 + low.astype(F32)).astype(jnp.int32)

    local_start = jnp.cumsum(count) - count
    present = count > 0
    odd_base = jnp.where(even, WINDOW - tok, WINDOW - 3 * tok)
    rest_base = jnp.where(even, WINDOW - 3 * tok, WINDOW - tok)

    def meta_of(before):
        return jnp.concatenate(
            [
                jnp.where(present, local_start, FAR),
                jnp.where(present, WINDOW + local_start - before, 0),
                jnp.stack([odd_base, rest_base]).astype(jnp.int32),
            ]
        )

    between = jnp.where(even | (count_of(two) == 0), 0, tok)
    before_near = count_of(two) + count_of(odd)
    meta_near = meta_of(before_near + between)
    m, acc = forward_near(meta_near, query_rows, kv, two, odd)
    m, four, weight_t = lax.optimization_barrier((m, four, weight_t))
    rest = swap(jnp.where(even, kv, four), "core")
    meta = meta_of(before_near + count_of(four) + count_of(rest))
    attn, lse = forward_far(meta, query_rows, four, rest, m, acc)

    weight_z = weight_t.reshape(n_z, -1, weight_t.shape[1])

    def weight_for(steps):
        return lax.dynamic_index_in_dim(weight_z, (z + steps) % n_z, 0, keepdims=False)

    weights = [weight_for(0)] + [z_shift(weight_for(s), s) for s in range(1, n_z)]
    attn_all = lax.all_gather(attn, "z", axis=0, tiled=True)

    core_1 = core.reshape(1).astype(jnp.int32)
    d_attn, dw_mine, dw_other = projection(core_1, out_grad, weight_t, attn, weight_z.shape[1])
    dw_other = swap(dw_other, "core")
    dw = (dw_mine.astype(F32) + dw_other.astype(F32)).astype(BF16)
    dw = lax.psum_scatter(dw, ("xl", "y"), scatter_dimension=0, tiled=True)
    weight_grad = lax.optimization_barrier(dw.astype(F32)).T

    common = (query_rows, d_attn, attn, lse)
    rest_part, four_part, dqt = backward(
        "attn_back_far", meta, common, (rest, four), (-9, WINDOW - 4 * tok)
    )
    rest_part = swap(rest_part, "core").astype(F32)
    four_sum = (four_part.astype(F32) + jnp.where(even, 0.0, rest_part)).astype(BF16)
    out_other = out_part("out_other", jnp.stack([1 - xh, z]), attn_all, weights)
    dqt, four_sum, out_other = lax.optimization_barrier((dqt, four_sum, out_other))
    four_sum = ctx_shift(four_sum, -4)
    out_other = swap(out_other, "xh")

    odd_part, two_part, dqt = backward(
        "attn_back_mid", meta, common, (odd, two), (-8, WINDOW - 2 * tok), dqt
    )
    odd_part = swap(odd_part, "core").astype(F32)
    two_sum = (two_part.astype(F32) + odd_part).astype(BF16)
    dqt, two_sum = lax.optimization_barrier((dqt, two_sum))
    two_sum = ctx_shift(two_sum, -2)

    own, query_grad = backward("attn_back_own", meta, common, (kv,), (WINDOW,), dqt, last=True)
    layer_out = out_part("out_mine", jnp.stack([xh, z]), attn_all, weights, (out_other,)).T

    own = own + jnp.where(even, rest_part, 0.0)
    own = (own + four_sum.astype(F32) + two_sum.astype(F32)).astype(BF16)
    return layer_out, query_grad, own[:, :HEAD_DIM], own[:, HEAD_DIM:], weight_grad


def solution(mesh):
    fine = Mesh(mesh.devices.reshape(2, 4, 2, 4, 2), CTX + FSDP)
    in_specs = (
        P(CTX, FSDP),
        P(CTX, FSDP),
        P(CTX, FSDP),
        P(CTX),
        P(FSDP, CTX),
        P(CTX, None),
    )
    out_specs = (
        P(CTX, FSDP),
        P(CTX, FSDP),
        P(CTX, FSDP),
        P(CTX, FSDP),
        P(FSDP, CTX),
    )
    return jax.shard_map(body, mesh=fine, in_specs=in_specs, out_specs=out_specs, check_vma=False)
```

```python
import functools
import math

import jax
import jax.numpy as jnp
from jax import lax
from jax.experimental import pallas as pl
from jax.experimental.pallas import tpu as pltpu
from jax.sharding import Mesh, PartitionSpec as P

HEAD_DIM = 128
WINDOW = 4096
N_DOCS = 4
SCALE = 1.0 / 12.0
SCALE2 = math.log2(math.e) / 12.0
NEG = -1e30
FAR = 1 << 30
F32 = jnp.float32
BF16 = jnp.bfloat16
NT = (((1,), (1,)), ((), ()))
NN = (((1,), (0,)), ((), ()))

TOK = 1024
BQ = 512
BK = 512
PROJ = 1152

CTX = ("xl", "y", "core")
FSDP = ("z", "xh")


def first_seen(meta, i):
    low = i + 1
    for d in range(N_DOCS):
        low = jnp.maximum(low, jnp.where(i >= meta[d], meta[N_DOCS + d], 0))
    return low


def heads_of(ref, q0):
    rows = pl.ds(q0, BQ)
    return jnp.concatenate([ref[rows, 0:HEAD_DIM], ref[rows, HEAD_DIM : 2 * HEAD_DIM]], 0)


def masked_tile(meta, tile, q0, place):
    i = q0 + lax.broadcasted_iota(jnp.int32, (1, BQ), 1)
    low = first_seen(meta, i) - place
    high = WINDOW + i - place
    row = lax.broadcasted_iota(jnp.int32, (BK, BQ), 0)
    seen = (row >= low) & (row <= high)
    return jnp.concatenate(
        [jnp.where(seen, tile[:, :BQ], NEG), jnp.where(seen, tile[:, BQ:], NEG)], 1
    )


def for_tiles(meta, q0, base, rows, tile):
    low_first = first_seen(meta, q0)
    low_last = first_seen(meta, q0 + BQ - 1)
    begin = jnp.maximum(low_first - base, 0) // BK
    end = jnp.minimum((WINDOW + q0 + BQ - 1 - base) // BK + 1, rows // BK)

    def step(t, carry):
        row = pl.multiple_of((end - 1 - t) * BK, BK)
        place = base + row
        plain = (place >= low_last) & (place + BK - 1 <= WINDOW + q0)

        @pl.when(plain)
        def _():
            tile(row, place, False)

        @pl.when(jnp.logical_not(plain))
        def _():
            tile(row, place, True)

        return carry

    lax.fori_loop(0, end - begin, step, 0)


def for_queries(tok, work):
    def step(t, carry):
        work(pl.multiple_of(t * BQ, BQ), pl.multiple_of(t * 2 * BQ, 2 * BQ))
        return carry

    lax.fori_loop(0, tok // BQ, step, 0)


def forward_tile(meta, q2, q0, k_ref, v_ref, m_ref, acc_ref, row, place, masked):
    k = k_ref[pl.ds(row, BK), :]
    v = v_ref[pl.ds(row, BK), :]
    s = lax.dot_general(k, q2, NT, preferred_element_type=F32)
    if masked:
        s = masked_tile(meta, s, q0, place)
    m_old = m_ref[0:1, :]
    m_new = jnp.maximum(m_old, jnp.max(s, axis=0, keepdims=True))
    p = jnp.exp2((s - m_new) * SCALE2)
    shrink = jnp.exp2((m_old - m_new) * SCALE2)
    v_ones = jnp.concatenate([v.T, jnp.ones((16, BK), BF16)], 0)
    acc_ref[...] = acc_ref[...] * shrink + lax.dot_general(
        v_ones, p.astype(BF16), NN, preferred_element_type=F32
    )
    m_ref[...] = jnp.broadcast_to(m_new, m_ref.shape)


def key_part(ref):
    return ref.at[:, 0:HEAD_DIM]


def value_part(ref):
    return ref.at[:, HEAD_DIM : 2 * HEAD_DIM]


def base_of(meta, base):
    return base if base >= 0 else meta[-base]


def forward_kernel(bases, first, last, meta, q_ref, *refs):
    n = len(bases)
    block_refs, refs = refs[:n], refs[n:]
    if not first:
        (m_in, acc_in), refs = refs[:2], refs[2:]
    one_out, two_out, m_ref, acc_ref = refs

    def work(q0, c0):
        cols = pl.ds(c0, 2 * BQ)
        q2 = heads_of(q_ref, q0)
        m_ref[...] = jnp.full(m_ref.shape, NEG, F32) if first else m_in[:, cols]
        acc_ref[...] = jnp.zeros(acc_ref.shape, F32) if first else acc_in[:, cols]
        for ref, base in zip(block_refs, bases):
            tile = functools.partial(
                forward_tile, meta, q2, q0, key_part(ref), value_part(ref), m_ref, acc_ref
            )
            for_tiles(meta, q0, base_of(meta, base), TOK, tile)
        if last:
            o = (acc_ref[0:HEAD_DIM, :] / acc_ref[HEAD_DIM : HEAD_DIM + 1, :]).T
            one_out[pl.ds(q0, BQ), 0:HEAD_DIM] = o[:BQ].astype(BF16)
            one_out[pl.ds(q0, BQ), HEAD_DIM : 2 * HEAD_DIM] = o[BQ:].astype(BF16)
            two_out[:, cols] = m_ref[...] * SCALE2 + jnp.log2(acc_ref[HEAD_DIM : HEAD_DIM + 8, :])
        else:
            one_out[:, cols] = m_ref[...]
            two_out[:, cols] = acc_ref[...]

    for_queries(TOK, work)


def forward(name, meta, q, blocks, bases, state=(), last=False):
    out = (
        jax.ShapeDtypeStruct((8, 2 * TOK), F32),
        jax.ShapeDtypeStruct((HEAD_DIM + 16, 2 * TOK), F32),
    )
    if last:
        out = (jax.ShapeDtypeStruct((TOK, 2 * HEAD_DIM), BF16), out[0])
    scratch = [pltpu.VMEM((8, 2 * BQ), F32), pltpu.VMEM((HEAD_DIM + 16, 2 * BQ), F32)]
    args = [q] + list(blocks) + list(state)
    kernel = functools.partial(forward_kernel, bases, not state, last)
    return call(kernel, name, len(args), out, scratch, 20)(meta, *args)


def call(kernel, name, n_vmem, out_shape, scratch, vmem_mb, cost=0):
    vmem = pl.BlockSpec(memory_space=pltpu.VMEM)
    return pl.pallas_call(
        kernel,
        out_shape=out_shape,
        in_specs=[pl.BlockSpec(memory_space=pltpu.SMEM)] + [vmem] * n_vmem,
        out_specs=jax.tree.map(lambda _: vmem, out_shape),
        scratch_shapes=scratch,
        compiler_params=pltpu.CompilerParams(vmem_limit_bytes=vmem_mb * 2**20),
        cost_estimate=pl.CostEstimate(flops=cost, bytes_accessed=0, transcendentals=0),
        name=name,
    )


def backward_kernel(bases, first, last, meta, q_ref, do_ref, o_ref, lse_ref, *refs):
    tok = q_ref.shape[0]
    n = len(bases)
    block_refs, refs = refs[:n], refs[n:]
    if not first:
        dqt_in, refs = refs[0], refs[1:]
    part_refs, dq_ref, (dqt, dk, dv) = refs[:n], refs[n], refs[n + 1 :]
    dk[...] = jnp.zeros(dk.shape, F32)
    dv[...] = jnp.zeros(dv.shape, F32)

    def work(q0, c0):
        cols = pl.ds(c0, 2 * BQ)
        q2 = heads_of(q_ref, q0)
        do2 = heads_of(do_ref, q0)
        o2 = heads_of(o_ref, q0)
        delta = jnp.sum((do2.astype(F32) * o2.astype(F32)).T, axis=0, keepdims=True)
        lse = lse_ref[0:1, cols]
        dqt[...] = jnp.zeros(dqt.shape, F32) if first else dqt_in[:, cols]

        def tile(index, row, place, masked):
            ref = block_refs[index]
            k = ref[pl.ds(row, BK), 0:HEAD_DIM]
            v = ref[pl.ds(row, BK), HEAD_DIM : 2 * HEAD_DIM]
            t = lax.dot_general(k, q2, NT, preferred_element_type=F32) * SCALE2 - lse
            if masked:
                t = masked_tile(meta, t, q0, place)
            p = jnp.exp2(t)
            dp = lax.dot_general(v, do2, NT, preferred_element_type=F32)
            ds = (p * (dp - delta)).astype(BF16)
            rows = pl.ds(row, BK)
            dv[index, rows, :] += lax.dot_general(
                p.astype(BF16), do2, NN, preferred_element_type=F32
            )
            dk[index, rows, :] += lax.dot_general(ds, q2, NN, preferred_element_type=F32)
            dqt[...] += lax.dot_general(k.T, ds, NN, preferred_element_type=F32)

        for index, base in enumerate(bases):
            for_tiles(meta, q0, base_of(meta, base), tok, functools.partial(tile, index))
        if last:
            dq = (dqt[...] * SCALE).T
            dq_ref[pl.ds(q0, BQ), 0:HEAD_DIM] = dq[:BQ].astype(BF16)
            dq_ref[pl.ds(q0, BQ), HEAD_DIM : 2 * HEAD_DIM] = dq[BQ:].astype(BF16)
        else:
            dq_ref[:, cols] = dqt[...]

    for_queries(tok, work)
    for index, ref in enumerate(part_refs):
        ref[:, 0:HEAD_DIM] = (dk[index] * SCALE).astype(ref.dtype)
        ref[:, HEAD_DIM : 2 * HEAD_DIM] = dv[index].astype(ref.dtype)


def backward(name, meta, common, blocks, bases, dqt=None, last=False):
    tok = common[0].shape[0]
    n = len(blocks)
    part = jax.ShapeDtypeStruct((tok, 2 * HEAD_DIM), F32 if last else BF16)
    dq = ((tok, 2 * HEAD_DIM), BF16) if last else ((HEAD_DIM, 2 * tok), F32)
    scratch = [
        pltpu.VMEM((HEAD_DIM, 2 * BQ), F32),
        pltpu.VMEM((n, tok, HEAD_DIM), F32),
        pltpu.VMEM((n, tok, HEAD_DIM), F32),
    ]
    args = list(common) + list(blocks) + ([] if dqt is None else [dqt])
    kernel = functools.partial(backward_kernel, bases, dqt is None, last)
    out = (part,) * n + (jax.ShapeDtypeStruct(*dq),)
    return call(kernel, name, len(args), out, scratch, 30)(meta, *args)


def projection_kernel(og_ref, wt_ref, attn_ref, d_attn_ref, dw_ref, total, attn_t):
    step = pl.program_id(0)

    @pl.when(step == 0)
    def _():
        total[...] = jnp.zeros(total.shape, F32)
        attn_t[...] = attn_ref[...].T

    og = og_ref[...]
    total[...] += lax.dot_general(og, wt_ref[...], NN, preferred_element_type=F32)
    dw_ref[...] = lax.dot_general(attn_t[...], og, NN, preferred_element_type=F32).T.astype(BF16)

    @pl.when(step == pl.num_programs(0) - 1)
    def _():
        d_attn_ref[...] = total[...].astype(BF16)


def projection(out_grad, weight_t, attn, chunk):
    tok, width = out_grad.shape
    heads = attn.shape[1]
    whole = pl.BlockSpec((tok, heads), lambda i: (0, 0))
    rows = pl.BlockSpec((chunk, heads), lambda i: (i, 0))
    return pl.pallas_call(
        projection_kernel,
        grid=(width // chunk,),
        out_shape=(
            jax.ShapeDtypeStruct((tok, heads), BF16),
            jax.ShapeDtypeStruct((width, heads), BF16),
        ),
        in_specs=[pl.BlockSpec((tok, chunk), lambda i: (0, i)), rows, whole],
        out_specs=(whole, rows),
        scratch_shapes=[pltpu.VMEM((tok, heads), F32), pltpu.VMEM((heads, tok), BF16)],
        compiler_params=pltpu.CompilerParams(vmem_limit_bytes=24 * 2**20),
        cost_estimate=pl.CostEstimate(flops=0, bytes_accessed=0, transcendentals=0),
        name="projection",
    )(out_grad, weight_t, attn)


def out_kernel(where, attn_ref, mine_ref, other_ref, *refs):
    n = attn_ref.shape[0] // TOK
    out_ref = refs[-1]
    cols = out_ref.shape[0]

    def with_weights(w_ref):
        total = refs[0][...].astype(F32) if len(refs) == 2 else None
        for steps in range(n):
            origin = lax.rem(where[1] + n - steps, n)
            a = attn_ref[pl.ds(pl.multiple_of(origin * TOK, TOK), TOK), :]
            w = w_ref[steps * cols : (steps + 1) * cols, :]
            term = lax.dot_general(w, a, NT, preferred_element_type=F32)
            total = term if total is None else total + term
        out_ref[...] = total.astype(BF16)

    @pl.when(where[0] == where[2])
    def _():
        with_weights(mine_ref)

    @pl.when(where[0] != where[2])
    def _():
        with_weights(other_ref)


def out_part(name, where, attn_all, mine, other, extra=()):
    args = [attn_all, mine, other] + list(extra)
    out = jax.ShapeDtypeStruct((mine.shape[0] // (attn_all.shape[0] // TOK), TOK), BF16)
    return call(out_kernel, name, len(args), out, [], 20)(where, *args)


def ctx_shift(value, steps):
    count = lax.axis_size(CTX)
    leading, last = max(0, -steps), min(count, count - steps)
    return lax.ppermute(value, CTX, [(s, s + steps) for s in range(leading, last)])


def swap(value, axis):
    return lax.ppermute(value, axis, [(0, 1), (1, 0)])


def z_shift(value, steps):
    count = lax.axis_size("z")
    return lax.ppermute(value, "z", [(s, (s + steps) % count) for s in range(count)])


def body(query_rows, key_rows, value_rows, doc_ids, out_weight, out_grad):
    tok = query_rows.shape[0]
    core = lax.axis_index("core")
    even = core == 0
    z = lax.axis_index("z")
    xh = lax.axis_index("xh")
    n_z = lax.axis_size("z")

    weight_t = lax.all_gather(out_weight.T, CTX, axis=0, tiled=True)

    docs = lax.iota(jnp.int32, N_DOCS)
    count = jnp.sum((doc_ids[None, :] == docs[:, None]).astype(jnp.int32), axis=1)
    info = jnp.stack([count // 32, count % 32]).astype(BF16)
    info = jnp.pad(info, ((0, 14), (0, 2 * HEAD_DIM - N_DOCS)))
    kv = jnp.concatenate([jnp.concatenate([key_rows, value_rows], 1), info], 0)
    two = ctx_shift(kv, 2)

    def count_of(block):
        high, low = block[tok, :N_DOCS], block[tok + 1, :N_DOCS]
        return (high.astype(F32) * 32 + low.astype(F32)).astype(jnp.int32)

    local_start = jnp.cumsum(count) - count
    present = count > 0
    odd_base = jnp.where(even, WINDOW - tok, WINDOW - 3 * tok)
    rest_base = jnp.where(even, WINDOW - 3 * tok, WINDOW - tok)

    def meta_of(before):
        return jnp.concatenate(
            [
                jnp.where(present, local_start, FAR),
                jnp.where(present, WINDOW + local_start - before, 0),
                jnp.stack([odd_base, rest_base]).astype(jnp.int32),
            ]
        )

    meta_own = meta_of(jnp.zeros_like(count))
    m, acc = forward("attn_own", meta_own, query_rows, (kv,), (WINDOW,))
    m, two = lax.optimization_barrier((m, two))
    odd = swap(two, "core")
    four = ctx_shift(two, 2)

    between = jnp.where(even | (count_of(two) == 0), 0, tok)
    before_near = count_of(two) + count_of(odd)
    meta_near = meta_of(before_near + between)
    m, acc = forward(
        "attn_near", meta_near, query_rows, (two, odd), (WINDOW - 2 * tok, -8), (m, acc)
    )
    m, four = lax.optimization_barrier((m, four))
    rest = swap(jnp.where(even, kv, four), "core")
    meta = meta_of(before_near + count_of(four) + count_of(rest))
    attn, lse = forward(
        "attn_far", meta, query_rows, (rest, four), (-9, WINDOW - 4 * tok), (m, acc), last=True
    )

    weight_z = weight_t.reshape(n_z, 2, -1, weight_t.shape[1])

    def weight_for(steps):
        half = lax.dynamic_slice(
            weight_z, ((z + steps) % n_z, core, 0, 0), (1, 1) + weight_z.shape[2:]
        )
        return half[0, 0]

    fetched = [z_shift(weight_for(s), s) for s in range(1, n_z)]
    attn_all = lax.all_gather(attn, "z", axis=0, tiled=True)

    d_attn, dw = projection(out_grad, weight_t, attn, PROJ)
    dw = lax.psum_scatter(dw, ("xl", "y"), scatter_dimension=0, tiled=True).reshape(2, -1, dw.shape[1])
    dw_mine = lax.dynamic_index_in_dim(dw, core, 0, keepdims=False)
    dw_other = swap(lax.dynamic_index_in_dim(dw, 1 - core, 0, keepdims=False), "core")
    weight_grad = lax.optimization_barrier(dw_mine.astype(F32) + dw_other.astype(F32)).T

    common = (query_rows, d_attn, attn, lse)
    rest_part, four_part, dqt = backward(
        "attn_back_far", meta, common, (rest, four), (-9, WINDOW - 4 * tok)
    )
    rest_part, fetched = lax.optimization_barrier((rest_part, fetched))
    w_mine = jnp.concatenate([weight_for(0)] + fetched, 0)
    w_other = swap(w_mine, "core")
    rest_part = swap(rest_part, "core").astype(F32)
    four_sum = (four_part.astype(F32) + jnp.where(even, 0.0, rest_part)).astype(BF16)
    out_other = out_part("out_other", jnp.stack([1 - xh, z, core]), attn_all, w_mine, w_other)
    dqt, four_sum, out_other = lax.optimization_barrier((dqt, four_sum, out_other))
    four_sum = ctx_shift(four_sum, -4)
    out_other = swap(out_other, "xh")

    odd_part, two_part, dqt = backward(
        "attn_back_mid", meta, common, (odd, two), (-8, WINDOW - 2 * tok), dqt
    )
    odd_part, four_sum = lax.optimization_barrier((odd_part, four_sum))
    odd_part = swap(odd_part, "core").astype(F32)
    two_sum = (two_part.astype(F32) + odd_part).astype(BF16)
    dqt, two_sum, out_other = lax.optimization_barrier((dqt, two_sum, out_other))
    two_sum = ctx_shift(two_sum, -2)

    own, query_grad = backward("attn_back_own", meta, common, (kv,), (WINDOW,), dqt, last=True)
    layer_out = out_part(
        "out_mine", jnp.stack([xh, z, core]), attn_all, w_mine, w_other, (out_other,)
    ).T

    own = own + jnp.where(even, rest_part, 0.0)
    own = (own + four_sum.astype(F32) + two_sum.astype(F32)).astype(BF16)
    return layer_out, query_grad, own[:, :HEAD_DIM], own[:, HEAD_DIM:], weight_grad


def solution(mesh):
    fine = Mesh(mesh.devices.reshape(2, 4, 2, 4, 2), CTX + FSDP)
    in_specs = (
        P(CTX, FSDP),
        P(CTX, FSDP),
        P(CTX, FSDP),
        P(CTX),
        P(FSDP, CTX),
        P(CTX, None),
    )
    out_specs = (
        P(CTX, FSDP),
        P(CTX, FSDP),
        P(CTX, FSDP),
        P(CTX, FSDP),
        P(FSDP, CTX),
    )
    return jax.shard_map(body, mesh=fine, in_specs=in_specs, out_specs=out_specs, check_vma=False)
```

```python
import functools
import math

import jax
import jax.numpy as jnp
from jax import lax
from jax.experimental import pallas as pl
from jax.experimental.pallas import tpu as pltpu
from jax.sharding import Mesh, PartitionSpec as P

HEAD_DIM = 128
WINDOW = 4096
N_DOCS = 4
SCALE = 1.0 / 12.0
SCALE2 = math.log2(math.e) / 12.0
NEG = -1e30
FAR = 1 << 30
F32 = jnp.float32
BF16 = jnp.bfloat16
NT = (((1,), (1,)), ((), ()))
NN = (((1,), (0,)), ((), ()))

TOK = 1024
BQ = 512
BK = 512
D_ROWS = 256
W_COLS = 1152

CTX = ("xl", "y", "core")
FSDP = ("z", "xh")


def first_seen(meta, i):
    low = i + 1
    for d in range(N_DOCS):
        low = jnp.maximum(low, jnp.where(i >= meta[d], meta[N_DOCS + d], 0))
    return low


def heads_of(ref, q0):
    rows = pl.ds(q0, BQ)
    return jnp.concatenate([ref[rows, 0:HEAD_DIM], ref[rows, HEAD_DIM : 2 * HEAD_DIM]], 0)


def masked_tile(meta, tile, q0, place):
    i = q0 + lax.broadcasted_iota(jnp.int32, (1, BQ), 1)
    low = first_seen(meta, i) - place
    high = WINDOW + i - place
    row = lax.broadcasted_iota(jnp.int32, (BK, BQ), 0)
    seen = (row >= low) & (row <= high)
    return jnp.concatenate(
        [jnp.where(seen, tile[:, :BQ], NEG), jnp.where(seen, tile[:, BQ:], NEG)], 1
    )


def for_tiles(meta, q0, base, rows, tile):
    low_first = first_seen(meta, q0)
    low_last = first_seen(meta, q0 + BQ - 1)
    begin = jnp.maximum(low_first - base, 0) // BK
    end = jnp.minimum((WINDOW + q0 + BQ - 1 - base) // BK + 1, rows // BK)

    def step(t, carry):
        row = pl.multiple_of((end - 1 - t) * BK, BK)
        place = base + row
        plain = (place >= low_last) & (place + BK - 1 <= WINDOW + q0)

        @pl.when(plain)
        def _():
            tile(row, place, False)

        @pl.when(jnp.logical_not(plain))
        def _():
            tile(row, place, True)

        return carry

    lax.fori_loop(0, end - begin, step, 0)


def for_queries(tok, work):
    def step(t, carry):
        work(pl.multiple_of(t * BQ, BQ), pl.multiple_of(t * 2 * BQ, 2 * BQ))
        return carry

    lax.fori_loop(0, tok // BQ, step, 0)


def forward_tile(meta, q2, q0, k_ref, v_ref, m_ref, acc_ref, row, place, masked):
    k = k_ref[pl.ds(row, BK), :]
    v = v_ref[pl.ds(row, BK), :]
    s = lax.dot_general(k, q2, NT, preferred_element_type=F32)
    if masked:
        s = masked_tile(meta, s, q0, place)
    m_old = m_ref[0:1, :]
    m_new = jnp.maximum(m_old, jnp.max(s, axis=0, keepdims=True))
    p = jnp.exp2((s - m_new) * SCALE2)
    shrink = jnp.exp2((m_old - m_new) * SCALE2)
    v_ones = jnp.concatenate([v.T, jnp.ones((16, BK), BF16)], 0)
    acc_ref[...] = acc_ref[...] * shrink + lax.dot_general(
        v_ones, p.astype(BF16), NN, preferred_element_type=F32
    )
    m_ref[...] = jnp.broadcast_to(m_new, m_ref.shape)


def key_part(ref):
    return ref.at[:, 0:HEAD_DIM]


def value_part(ref):
    return ref.at[:, HEAD_DIM : 2 * HEAD_DIM]


def base_of(meta, base):
    return base if base >= 0 else meta[-base]


def forward_kernel(bases, first, last, meta, q_ref, *refs):
    n = len(bases)
    block_refs, refs = refs[:n], refs[n:]
    if not first:
        (m_in, acc_in), refs = refs[:2], refs[2:]
    one_out, two_out, m_ref, acc_ref = refs

    def work(q0, c0):
        cols = pl.ds(c0, 2 * BQ)
        q2 = heads_of(q_ref, q0)
        m_ref[...] = jnp.full(m_ref.shape, NEG, F32) if first else m_in[:, cols]
        acc_ref[...] = jnp.zeros(acc_ref.shape, F32) if first else acc_in[:, cols]
        for ref, base in zip(block_refs, bases):
            tile = functools.partial(
                forward_tile, meta, q2, q0, key_part(ref), value_part(ref), m_ref, acc_ref
            )
            for_tiles(meta, q0, base_of(meta, base), TOK, tile)
        if last:
            o = (acc_ref[0:HEAD_DIM, :] / acc_ref[HEAD_DIM : HEAD_DIM + 1, :]).T
            one_out[pl.ds(q0, BQ), 0:HEAD_DIM] = o[:BQ].astype(BF16)
            one_out[pl.ds(q0, BQ), HEAD_DIM : 2 * HEAD_DIM] = o[BQ:].astype(BF16)
            two_out[:, cols] = m_ref[...] * SCALE2 + jnp.log2(acc_ref[HEAD_DIM : HEAD_DIM + 8, :])
        else:
            one_out[:, cols] = m_ref[...]
            two_out[:, cols] = acc_ref[...]

    for_queries(TOK, work)


def forward(name, meta, q, blocks, bases, state=(), last=False):
    out = (
        jax.ShapeDtypeStruct((8, 2 * TOK), F32),
        jax.ShapeDtypeStruct((HEAD_DIM + 16, 2 * TOK), F32),
    )
    if last:
        out = (jax.ShapeDtypeStruct((TOK, 2 * HEAD_DIM), BF16), out[0])
    scratch = [pltpu.VMEM((8, 2 * BQ), F32), pltpu.VMEM((HEAD_DIM + 16, 2 * BQ), F32)]
    args = [q] + list(blocks) + list(state)
    kernel = functools.partial(forward_kernel, bases, not state, last)
    return call(kernel, name, len(args), out, scratch, 20)(meta, *args)


def call(kernel, name, n_vmem, out_shape, scratch, vmem_mb, cost=0):
    vmem = pl.BlockSpec(memory_space=pltpu.VMEM)
    return pl.pallas_call(
        kernel,
        out_shape=out_shape,
        in_specs=[pl.BlockSpec(memory_space=pltpu.SMEM)] + [vmem] * n_vmem,
        out_specs=jax.tree.map(lambda _: vmem, out_shape),
        scratch_shapes=scratch,
        compiler_params=pltpu.CompilerParams(vmem_limit_bytes=vmem_mb * 2**20),
        cost_estimate=pl.CostEstimate(flops=cost, bytes_accessed=0, transcendentals=0),
        name=name,
    )


def backward_kernel(bases, first, last, meta, q_ref, do_ref, o_ref, lse_ref, *refs):
    tok = q_ref.shape[0]
    n = len(bases)
    block_refs, refs = refs[:n], refs[n:]
    if not first:
        dqt_in, refs = refs[0], refs[1:]
    part_refs, dq_ref, (dqt, dk, dv) = refs[:n], refs[n], refs[n + 1 :]
    dk[...] = jnp.zeros(dk.shape, F32)
    dv[...] = jnp.zeros(dv.shape, F32)

    def work(q0, c0):
        cols = pl.ds(c0, 2 * BQ)
        q2 = heads_of(q_ref, q0)
        do2 = heads_of(do_ref, q0)
        o2 = heads_of(o_ref, q0)
        delta = jnp.sum((do2.astype(F32) * o2.astype(F32)).T, axis=0, keepdims=True)
        lse = lse_ref[0:1, cols]
        dqt[...] = jnp.zeros(dqt.shape, F32) if first else dqt_in[:, cols]

        def tile(index, row, place, masked):
            ref = block_refs[index]
            k = ref[pl.ds(row, BK), 0:HEAD_DIM]
            v = ref[pl.ds(row, BK), HEAD_DIM : 2 * HEAD_DIM]
            t = lax.dot_general(k, q2, NT, preferred_element_type=F32) * SCALE2 - lse
            if masked:
                t = masked_tile(meta, t, q0, place)
            p = jnp.exp2(t)
            dp = lax.dot_general(v, do2, NT, preferred_element_type=F32)
            ds = (p * (dp - delta)).astype(BF16)
            rows = pl.ds(row, BK)
            dv[index, rows, :] += lax.dot_general(
                p.astype(BF16), do2, NN, preferred_element_type=F32
            )
            dk[index, rows, :] += lax.dot_general(ds, q2, NN, preferred_element_type=F32)
            dqt[...] += lax.dot_general(k.T, ds, NN, preferred_element_type=F32)

        for index, base in enumerate(bases):
            for_tiles(meta, q0, base_of(meta, base), tok, functools.partial(tile, index))
        if last:
            dq = (dqt[...] * SCALE).T
            dq_ref[pl.ds(q0, BQ), 0:HEAD_DIM] = dq[:BQ].astype(BF16)
            dq_ref[pl.ds(q0, BQ), HEAD_DIM : 2 * HEAD_DIM] = dq[BQ:].astype(BF16)
        else:
            dq_ref[:, cols] = dqt[...]

    for_queries(tok, work)
    for index, ref in enumerate(part_refs):
        ref[:, 0:HEAD_DIM] = (dk[index] * SCALE).astype(ref.dtype)
        ref[:, HEAD_DIM : 2 * HEAD_DIM] = dv[index].astype(ref.dtype)


def backward(name, meta, common, blocks, bases, dqt=None, last=False):
    tok = common[0].shape[0]
    n = len(blocks)
    part = jax.ShapeDtypeStruct((tok, 2 * HEAD_DIM), F32 if last else BF16)
    dq = ((tok, 2 * HEAD_DIM), BF16) if last else ((HEAD_DIM, 2 * tok), F32)
    scratch = [
        pltpu.VMEM((HEAD_DIM, 2 * BQ), F32),
        pltpu.VMEM((n, tok, HEAD_DIM), F32),
        pltpu.VMEM((n, tok, HEAD_DIM), F32),
    ]
    args = list(common) + list(blocks) + ([] if dqt is None else [dqt])
    kernel = functools.partial(backward_kernel, bases, dqt is None, last)
    out = (part,) * n + (jax.ShapeDtypeStruct(*dq),)
    return call(kernel, name, len(args), out, scratch, 30)(meta, *args)


def d_attn_kernel(og_ref, wt_ref, out_ref):
    out_ref[...] = lax.dot_general(
        og_ref[...], wt_ref[...], NN, preferred_element_type=F32
    ).astype(BF16)


def weight_grad_kernel(og_ref, attn_ref, out_ref, attn_t):
    @pl.when(pl.program_id(0) == 0)
    def _():
        attn_t[...] = attn_ref[...].T

    out_ref[...] = lax.dot_general(
        attn_t[...], og_ref[...], NN, preferred_element_type=F32
    ).T.astype(BF16)


def streamed(kernel, name, steps, in_specs, out_spec, out_shape, scratch):
    return pl.pallas_call(
        kernel,
        grid=(steps,),
        out_shape=out_shape,
        in_specs=in_specs,
        out_specs=out_spec,
        scratch_shapes=scratch,
        compiler_params=pltpu.CompilerParams(vmem_limit_bytes=58 * 2**20),
        cost_estimate=pl.CostEstimate(flops=0, bytes_accessed=0, transcendentals=0),
        name=name,
    )


def d_attn_of(out_grad, weight_t):
    tok, width = out_grad.shape
    heads = weight_t.shape[1]
    in_specs = [
        pl.BlockSpec((D_ROWS, width), lambda i: (i, 0)),
        pl.BlockSpec((width, heads), lambda i: (0, 0)),
    ]
    out_spec = pl.BlockSpec((D_ROWS, heads), lambda i: (i, 0))
    out = jax.ShapeDtypeStruct((tok, heads), BF16)
    return streamed(d_attn_kernel, "d_attn", tok // D_ROWS, in_specs, out_spec, out, [])(
        out_grad, weight_t
    )


def weight_grad_of(out_grad, attn):
    tok, width = out_grad.shape
    heads = attn.shape[1]
    in_specs = [
        pl.BlockSpec((tok, W_COLS), lambda i: (0, i)),
        pl.BlockSpec((tok, heads), lambda i: (0, 0)),
    ]
    out_spec = pl.BlockSpec((W_COLS, heads), lambda i: (i, 0))
    out = jax.ShapeDtypeStruct((width, heads), BF16)
    scratch = [pltpu.VMEM((heads, tok), BF16)]
    return streamed(
        weight_grad_kernel, "weight_grad", width // W_COLS, in_specs, out_spec, out, scratch
    )(out_grad, attn)


def out_kernel(n, where, mine_ref, other_ref, *refs):
    attn_refs, refs = refs[:n], refs[n:]
    out_ref = refs[-1]
    cols = out_ref.shape[0]

    def with_weights(w_ref):
        total = refs[0][...].astype(F32) if len(refs) == 2 else None
        for i, a_ref in enumerate(attn_refs):
            w = w_ref[i * cols : (i + 1) * cols, :]
            term = lax.dot_general(w, a_ref[...], NT, preferred_element_type=F32)
            total = term if total is None else total + term
        out_ref[...] = total.astype(BF16)

    @pl.when(where[0] == where[1])
    def _():
        with_weights(mine_ref)

    @pl.when(where[0] != where[1])
    def _():
        with_weights(other_ref)


def out_part(name, where, attns, mine, other, extra=()):
    args = [mine, other] + list(attns) + list(extra)
    out = jax.ShapeDtypeStruct((mine.shape[0] // len(attns), TOK), BF16)
    kernel = functools.partial(out_kernel, len(attns))
    return call(kernel, name, len(args), out, [], 20)(where, *args)


def ctx_shift(value, steps):
    count = lax.axis_size(CTX)
    leading, last = max(0, -steps), min(count, count - steps)
    return lax.ppermute(value, CTX, [(s, s + steps) for s in range(leading, last)])


def swap(value, axis):
    return lax.ppermute(value, axis, [(0, 1), (1, 0)])


def z_shift(value, steps):
    count = lax.axis_size("z")
    return lax.ppermute(value, "z", [(s, (s + steps) % count) for s in range(count)])


def body(query_rows, key_rows, value_rows, doc_ids, out_weight, out_grad):
    tok = query_rows.shape[0]
    core = lax.axis_index("core")
    even = core == 0
    z = lax.axis_index("z")
    xh = lax.axis_index("xh")
    n_z = lax.axis_size("z")

    weight_t = lax.all_gather(out_weight.T, CTX, axis=0, tiled=True)

    docs = lax.iota(jnp.int32, N_DOCS)
    count = jnp.sum((doc_ids[None, :] == docs[:, None]).astype(jnp.int32), axis=1)
    info = jnp.stack([count // 32, count % 32]).astype(BF16)
    info = jnp.pad(info, ((0, 14), (0, 2 * HEAD_DIM - N_DOCS)))
    kv = jnp.concatenate([jnp.concatenate([key_rows, value_rows], 1), info], 0)
    two = ctx_shift(kv, 2)

    def count_of(block):
        high, low = block[tok, :N_DOCS], block[tok + 1, :N_DOCS]
        return (high.astype(F32) * 32 + low.astype(F32)).astype(jnp.int32)

    local_start = jnp.cumsum(count) - count
    present = count > 0
    odd_base = jnp.where(even, WINDOW - tok, WINDOW - 3 * tok)
    rest_base = jnp.where(even, WINDOW - 3 * tok, WINDOW - tok)

    def meta_of(before):
        return jnp.concatenate(
            [
                jnp.where(present, local_start, FAR),
                jnp.where(present, WINDOW + local_start - before, 0),
                jnp.stack([odd_base, rest_base]).astype(jnp.int32),
            ]
        )

    meta_own = meta_of(jnp.zeros_like(count))
    m, acc = forward("attn_own", meta_own, query_rows, (kv,), (WINDOW,))
    m, two = lax.optimization_barrier((m, two))
    odd = swap(two, "core")
    four = ctx_shift(two, 2)

    between = jnp.where(even | (count_of(two) == 0), 0, tok)
    before_near = count_of(two) + count_of(odd)
    meta_near = meta_of(before_near + between)
    m, acc = forward(
        "attn_near", meta_near, query_rows, (two, odd), (WINDOW - 2 * tok, -8), (m, acc)
    )
    m, four, weight_t = lax.optimization_barrier((m, four, weight_t))
    rest = swap(jnp.where(even, kv, four), "core")
    meta = meta_of(before_near + count_of(four) + count_of(rest))

    weight_z = weight_t.reshape(n_z, 2, -1, weight_t.shape[1])

    def weight_for(steps):
        half = lax.dynamic_slice(
            weight_z, ((z + steps) % n_z, core, 0, 0), (1, 1) + weight_z.shape[2:]
        )
        return half[0, 0]

    fetched = [z_shift(weight_for(s), s) for s in range(1, n_z)]
    d_attn = d_attn_of(out_grad, weight_t)
    m, d_attn = lax.optimization_barrier((m, d_attn))
    attn, lse = forward(
        "attn_far", meta, query_rows, (rest, four), (-9, WINDOW - 4 * tok), (m, acc), last=True
    )
    attns = [attn] + [z_shift(attn, s) for s in range(1, n_z)]
    attn, fetched = lax.optimization_barrier((attn, fetched))
    w_mine = jnp.concatenate([weight_for(0)] + fetched, 0)
    w_other = swap(w_mine, "core")

    dw = weight_grad_of(out_grad, attn)
    dw = lax.psum_scatter(dw, ("xl", "y"), scatter_dimension=0, tiled=True).reshape(2, -1, dw.shape[1])
    dw_mine = lax.dynamic_index_in_dim(dw, core, 0, keepdims=False)
    dw_other = swap(lax.dynamic_index_in_dim(dw, 1 - core, 0, keepdims=False), "core")
    weight_grad = lax.optimization_barrier(dw_mine.astype(F32) + dw_other.astype(F32)).T

    common = (query_rows, d_attn, attn, lse)
    rest_part, four_part, dqt = backward(
        "attn_back_far", meta, common, (rest, four), (-9, WINDOW - 4 * tok)
    )
    rest_part, attns = lax.optimization_barrier((rest_part, attns))
    rest_part = swap(rest_part, "core").astype(F32)
    four_sum = (four_part.astype(F32) + jnp.where(even, 0.0, rest_part)).astype(BF16)
    out_other = out_part("out_other", jnp.stack([1 - xh, core]), attns, w_mine, w_other)
    dqt, four_sum, out_other = lax.optimization_barrier((dqt, four_sum, out_other))
    four_sum = ctx_shift(four_sum, -2)
    out_other = swap(out_other, "xh")

    odd_part, two_part, dqt = backward(
        "attn_back_mid", meta, common, (odd, two), (-8, WINDOW - 2 * tok), dqt
    )
    odd_part, four_sum = lax.optimization_barrier((odd_part, four_sum))
    odd_part = swap(odd_part, "core").astype(F32)
    two_sum = (two_part.astype(F32) + odd_part + four_sum.astype(F32)).astype(BF16)
    dqt, two_sum, out_other = lax.optimization_barrier((dqt, two_sum, out_other))
    two_sum = ctx_shift(two_sum, -2)

    own, query_grad = backward("attn_back_own", meta, common, (kv,), (WINDOW,), dqt, last=True)
    layer_out = out_part(
        "out_mine", jnp.stack([xh, core]), attns, w_mine, w_other, (out_other,)
    ).T

    own = own + jnp.where(even, rest_part, 0.0)
    own = (own + two_sum.astype(F32)).astype(BF16)
    return layer_out, query_grad, own[:, :HEAD_DIM], own[:, HEAD_DIM:], weight_grad


def solution(mesh):
    fine = Mesh(mesh.devices.reshape(2, 4, 2, 4, 2), CTX + FSDP)
    in_specs = (
        P(CTX, FSDP),
        P(CTX, FSDP),
        P(CTX, FSDP),
        P(CTX),
        P(FSDP, CTX),
        P(CTX, None),
    )
    out_specs = (
        P(CTX, FSDP),
        P(CTX, FSDP),
        P(CTX, FSDP),
        P(CTX, FSDP),
        P(FSDP, CTX),
    )
    return jax.shard_map(body, mesh=fine, in_specs=in_specs, out_specs=out_specs, check_vma=False)
```

```python
import functools
import math

import jax
import jax.numpy as jnp
from jax import lax
from jax.experimental import pallas as pl
from jax.experimental.pallas import tpu as pltpu
from jax.sharding import Mesh, PartitionSpec as P

HEAD_DIM = 128
WINDOW = 4096
N_DOCS = 4
SCALE = 1.0 / 12.0
SCALE2 = math.log2(math.e) / 12.0
NEG = -1e30
FAR = 1 << 30
F32 = jnp.float32
BF16 = jnp.bfloat16
NT = (((1,), (1,)), ((), ()))
NN = (((1,), (0,)), ((), ()))

TOK = 1024
BQ = 512
BK = 512
D_ROWS = 256
W_COLS = 1152

CTX = ("xl", "y", "core")
FSDP = ("z", "xh")


def first_seen(meta, i):
    low = i + 1
    for d in range(N_DOCS):
        low = jnp.maximum(low, jnp.where(i >= meta[d], meta[N_DOCS + d], 0))
    return low


def heads_of(ref, q0):
    rows = pl.ds(q0, BQ)
    return jnp.concatenate([ref[rows, 0:HEAD_DIM], ref[rows, HEAD_DIM : 2 * HEAD_DIM]], 0)


def masked_tile(meta, tile, q0, place):
    i = q0 + lax.broadcasted_iota(jnp.int32, (1, BQ), 1)
    low = first_seen(meta, i) - place
    high = WINDOW + i - place
    row = lax.broadcasted_iota(jnp.int32, (BK, BQ), 0)
    seen = (row >= low) & (row <= high)
    return jnp.concatenate(
        [jnp.where(seen, tile[:, :BQ], NEG), jnp.where(seen, tile[:, BQ:], NEG)], 1
    )


def for_tiles(meta, q0, base, rows, tile):
    low_first = first_seen(meta, q0)
    low_last = first_seen(meta, q0 + BQ - 1)
    begin = jnp.maximum(low_first - base, 0) // BK
    end = jnp.minimum((WINDOW + q0 + BQ - 1 - base) // BK + 1, rows // BK)

    def step(t, carry):
        row = pl.multiple_of((end - 1 - t) * BK, BK)
        place = base + row
        plain = (place >= low_last) & (place + BK - 1 <= WINDOW + q0)

        @pl.when(plain)
        def _():
            tile(row, place, False)

        @pl.when(jnp.logical_not(plain))
        def _():
            tile(row, place, True)

        return carry

    lax.fori_loop(0, end - begin, step, 0)


def for_queries(tok, work):
    def step(t, carry):
        work(pl.multiple_of(t * BQ, BQ), pl.multiple_of(t * 2 * BQ, 2 * BQ))
        return carry

    lax.fori_loop(0, tok // BQ, step, 0)


def forward_tile(meta, q2, q0, k_ref, v_ref, m_ref, acc_ref, row, place, masked):
    k = k_ref[pl.ds(row, BK), :]
    v = v_ref[pl.ds(row, BK), :]
    s = lax.dot_general(k, q2, NT, preferred_element_type=F32)
    if masked:
        s = masked_tile(meta, s, q0, place)
    m_old = m_ref[0:1, :]
    m_new = jnp.maximum(m_old, jnp.max(s, axis=0, keepdims=True))
    p = jnp.exp2((s - m_new) * SCALE2)
    shrink = jnp.exp2((m_old - m_new) * SCALE2)
    v_ones = jnp.concatenate([v.T, jnp.ones((16, BK), BF16)], 0)
    acc_ref[...] = acc_ref[...] * shrink + lax.dot_general(
        v_ones, p.astype(BF16), NN, preferred_element_type=F32
    )
    m_ref[...] = jnp.broadcast_to(m_new, m_ref.shape)


def key_part(ref):
    return ref.at[:, 0:HEAD_DIM]


def value_part(ref):
    return ref.at[:, HEAD_DIM : 2 * HEAD_DIM]


def base_of(meta, base):
    return base if base >= 0 else meta[-base]


def forward_kernel(bases, first, last, meta, q_ref, *refs):
    n = len(bases)
    block_refs, refs = refs[:n], refs[n:]
    if not first:
        (m_in, acc_in), refs = refs[:2], refs[2:]
    one_out, two_out, m_ref, acc_ref = refs

    def work(q0, c0):
        cols = pl.ds(c0, 2 * BQ)
        q2 = heads_of(q_ref, q0)
        m_ref[...] = jnp.full(m_ref.shape, NEG, F32) if first else m_in[:, cols]
        acc_ref[...] = jnp.zeros(acc_ref.shape, F32) if first else acc_in[:, cols]
        for ref, base in zip(block_refs, bases):
            tile = functools.partial(
                forward_tile, meta, q2, q0, key_part(ref), value_part(ref), m_ref, acc_ref
            )
            for_tiles(meta, q0, base_of(meta, base), TOK, tile)
        if last:
            o = (acc_ref[0:HEAD_DIM, :] / acc_ref[HEAD_DIM : HEAD_DIM + 1, :]).T
            one_out[pl.ds(q0, BQ), 0:HEAD_DIM] = o[:BQ].astype(BF16)
            one_out[pl.ds(q0, BQ), HEAD_DIM : 2 * HEAD_DIM] = o[BQ:].astype(BF16)
            two_out[:, cols] = m_ref[...] * SCALE2 + jnp.log2(acc_ref[HEAD_DIM : HEAD_DIM + 8, :])
        else:
            one_out[:, cols] = m_ref[...]
            two_out[:, cols] = acc_ref[...]

    for_queries(TOK, work)


def forward(name, meta, q, blocks, bases, state=(), last=False):
    out = (
        jax.ShapeDtypeStruct((8, 2 * TOK), F32),
        jax.ShapeDtypeStruct((HEAD_DIM + 16, 2 * TOK), F32),
    )
    if last:
        out = (jax.ShapeDtypeStruct((TOK, 2 * HEAD_DIM), BF16), out[0])
    scratch = [pltpu.VMEM((8, 2 * BQ), F32), pltpu.VMEM((HEAD_DIM + 16, 2 * BQ), F32)]
    args = [q] + list(blocks) + list(state)
    kernel = functools.partial(forward_kernel, bases, not state, last)
    return call(kernel, name, len(args), out, scratch, 20)(meta, *args)


def call(kernel, name, n_vmem, out_shape, scratch, vmem_mb, cost=0):
    vmem = pl.BlockSpec(memory_space=pltpu.VMEM)
    return pl.pallas_call(
        kernel,
        out_shape=out_shape,
        in_specs=[pl.BlockSpec(memory_space=pltpu.SMEM)] + [vmem] * n_vmem,
        out_specs=jax.tree.map(lambda _: vmem, out_shape),
        scratch_shapes=scratch,
        compiler_params=pltpu.CompilerParams(vmem_limit_bytes=vmem_mb * 2**20),
        cost_estimate=pl.CostEstimate(flops=cost, bytes_accessed=0, transcendentals=0),
        name=name,
    )


def backward_kernel(bases, first, last, meta, q_ref, do_ref, o_ref, lse_ref, *refs):
    tok = q_ref.shape[0]
    n = len(bases)
    block_refs, refs = refs[:n], refs[n:]
    if not first:
        dqt_in, refs = refs[0], refs[1:]
    part_refs, dq_ref, (dqt, dk, dv) = refs[:n], refs[n], refs[n + 1 :]
    dk[...] = jnp.zeros(dk.shape, F32)
    dv[...] = jnp.zeros(dv.shape, F32)

    def work(q0, c0):
        cols = pl.ds(c0, 2 * BQ)
        q2 = heads_of(q_ref, q0)
        do2 = heads_of(do_ref, q0)
        o2 = heads_of(o_ref, q0)
        delta = jnp.sum((do2.astype(F32) * o2.astype(F32)).T, axis=0, keepdims=True)
        lse = lse_ref[0:1, cols]
        dqt[...] = jnp.zeros(dqt.shape, F32) if first else dqt_in[:, cols]

        def tile(index, row, place, masked):
            ref = block_refs[index]
            k = ref[pl.ds(row, BK), 0:HEAD_DIM]
            v = ref[pl.ds(row, BK), HEAD_DIM : 2 * HEAD_DIM]
            t = lax.dot_general(k, q2, NT, preferred_element_type=F32) * SCALE2 - lse
            if masked:
                t = masked_tile(meta, t, q0, place)
            p = jnp.exp2(t)
            dp = lax.dot_general(v, do2, NT, preferred_element_type=F32)
            ds = (p * (dp - delta)).astype(BF16)
            rows = pl.ds(row, BK)
            dv[index, rows, :] += lax.dot_general(
                p.astype(BF16), do2, NN, preferred_element_type=F32
            )
            dk[index, rows, :] += lax.dot_general(ds, q2, NN, preferred_element_type=F32)
            dqt[...] += lax.dot_general(k.T, ds, NN, preferred_element_type=F32)

        for index, base in enumerate(bases):
            for_tiles(meta, q0, base_of(meta, base), tok, functools.partial(tile, index))
        if last:
            dq = (dqt[...] * SCALE).T
            dq_ref[pl.ds(q0, BQ), 0:HEAD_DIM] = dq[:BQ].astype(BF16)
            dq_ref[pl.ds(q0, BQ), HEAD_DIM : 2 * HEAD_DIM] = dq[BQ:].astype(BF16)
        else:
            dq_ref[:, cols] = dqt[...]

    for_queries(tok, work)
    for index, ref in enumerate(part_refs):
        ref[:, 0:HEAD_DIM] = (dk[index] * SCALE).astype(ref.dtype)
        ref[:, HEAD_DIM : 2 * HEAD_DIM] = dv[index].astype(ref.dtype)


def backward(name, meta, common, blocks, bases, dqt=None, last=False):
    tok = common[0].shape[0]
    n = len(blocks)
    part = jax.ShapeDtypeStruct((tok, 2 * HEAD_DIM), F32 if last else BF16)
    dq = ((tok, 2 * HEAD_DIM), BF16) if last else ((HEAD_DIM, 2 * tok), F32)
    scratch = [
        pltpu.VMEM((HEAD_DIM, 2 * BQ), F32),
        pltpu.VMEM((n, tok, HEAD_DIM), F32),
        pltpu.VMEM((n, tok, HEAD_DIM), F32),
    ]
    args = list(common) + list(blocks) + ([] if dqt is None else [dqt])
    kernel = functools.partial(backward_kernel, bases, dqt is None, last)
    out = (part,) * n + (jax.ShapeDtypeStruct(*dq),)
    cost = 0 if dqt is None or last else 40_000_000_000
    return call(kernel, name, len(args), out, scratch, 30, cost)(meta, *args)


def d_attn_kernel(og_ref, wt_ref, out_ref):
    out_ref[...] = lax.dot_general(
        og_ref[...], wt_ref[...], NN, preferred_element_type=F32
    ).astype(BF16)


def weight_grad_kernel(og_ref, attn_ref, out_ref, attn_t):
    @pl.when(pl.program_id(0) == 0)
    def _():
        attn_t[...] = attn_ref[...].T

    out_ref[...] = lax.dot_general(
        attn_t[...], og_ref[...], NN, preferred_element_type=F32
    ).T.astype(BF16)


def streamed(kernel, name, steps, in_specs, out_spec, out_shape, scratch):
    return pl.pallas_call(
        kernel,
        grid=(steps,),
        out_shape=out_shape,
        in_specs=in_specs,
        out_specs=out_spec,
        scratch_shapes=scratch,
        compiler_params=pltpu.CompilerParams(vmem_limit_bytes=58 * 2**20),
        cost_estimate=pl.CostEstimate(flops=0, bytes_accessed=0, transcendentals=0),
        name=name,
    )


def d_attn_of(out_grad, weight_t):
    tok, width = out_grad.shape
    heads = weight_t.shape[1]
    in_specs = [
        pl.BlockSpec((D_ROWS, width), lambda i: (i, 0)),
        pl.BlockSpec((width, heads), lambda i: (0, 0)),
    ]
    out_spec = pl.BlockSpec((D_ROWS, heads), lambda i: (i, 0))
    out = jax.ShapeDtypeStruct((tok, heads), BF16)
    return streamed(d_attn_kernel, "d_attn", tok // D_ROWS, in_specs, out_spec, out, [])(
        out_grad, weight_t
    )


def weight_grad_of(out_grad, attn):
    tok, width = out_grad.shape
    heads = attn.shape[1]
    in_specs = [
        pl.BlockSpec((tok, W_COLS), lambda i: (0, i)),
        pl.BlockSpec((tok, heads), lambda i: (0, 0)),
    ]
    out_spec = pl.BlockSpec((W_COLS, heads), lambda i: (i, 0))
    out = jax.ShapeDtypeStruct((width, heads), BF16)
    scratch = [pltpu.VMEM((heads, tok), BF16)]
    return streamed(
        weight_grad_kernel, "weight_grad", width // W_COLS, in_specs, out_spec, out, scratch
    )(out_grad, attn)


def out_kernel(n, where, mine_ref, other_ref, *refs):
    attn_refs, refs = refs[:n], refs[n:]
    out_ref = refs[-1]
    cols = out_ref.shape[0]

    def with_weights(w_ref):
        total = refs[0][...].astype(F32) if len(refs) == 2 else None
        for i, a_ref in enumerate(attn_refs):
            w = w_ref[i * cols : (i + 1) * cols, :]
            term = lax.dot_general(w, a_ref[...], NT, preferred_element_type=F32)
            total = term if total is None else total + term
        out_ref[...] = total.astype(BF16)

    @pl.when(where[0] == where[1])
    def _():
        with_weights(mine_ref)

    @pl.when(where[0] != where[1])
    def _():
        with_weights(other_ref)


def out_part(name, where, attns, mine, other, extra=()):
    args = [mine, other] + list(attns) + list(extra)
    out = jax.ShapeDtypeStruct((mine.shape[0] // len(attns), TOK), BF16)
    kernel = functools.partial(out_kernel, len(attns))
    return call(kernel, name, len(args), out, [], 20)(where, *args)


def ctx_shift(value, steps):
    count = lax.axis_size(CTX)
    leading, last = max(0, -steps), min(count, count - steps)
    return lax.ppermute(value, CTX, [(s, s + steps) for s in range(leading, last)])


def swap(value, axis):
    return lax.ppermute(value, axis, [(0, 1), (1, 0)])


def z_shift(value, steps):
    count = lax.axis_size("z")
    return lax.ppermute(value, "z", [(s, (s + steps) % count) for s in range(count)])


def body(query_rows, key_rows, value_rows, doc_ids, out_weight, out_grad):
    tok = query_rows.shape[0]
    core = lax.axis_index("core")
    even = core == 0
    z = lax.axis_index("z")
    xh = lax.axis_index("xh")
    n_z = lax.axis_size("z")

    weight_t = lax.all_gather(out_weight.T, CTX, axis=0, tiled=True)

    docs = lax.iota(jnp.int32, N_DOCS)
    count = jnp.sum((doc_ids[None, :] == docs[:, None]).astype(jnp.int32), axis=1)
    info = jnp.stack([count // 32, count % 32]).astype(BF16)
    info = jnp.pad(info, ((0, 14), (0, 2 * HEAD_DIM - N_DOCS)))
    kv = jnp.concatenate([jnp.concatenate([key_rows, value_rows], 1), info], 0)
    two = ctx_shift(kv, 2)

    def count_of(block):
        high, low = block[tok, :N_DOCS], block[tok + 1, :N_DOCS]
        return (high.astype(F32) * 32 + low.astype(F32)).astype(jnp.int32)

    local_start = jnp.cumsum(count) - count
    present = count > 0
    odd_base = jnp.where(even, WINDOW - tok, WINDOW - 3 * tok)
    rest_base = jnp.where(even, WINDOW - 3 * tok, WINDOW - tok)

    def meta_of(before):
        return jnp.concatenate(
            [
                jnp.where(present, local_start, FAR),
                jnp.where(present, WINDOW + local_start - before, 0),
                jnp.stack([odd_base, rest_base]).astype(jnp.int32),
            ]
        )

    meta_own = meta_of(jnp.zeros_like(count))
    m, acc = forward("attn_own", meta_own, query_rows, (kv,), (WINDOW,))
    m, two = lax.optimization_barrier((m, two))
    odd = swap(two, "core")
    four = ctx_shift(two, 2)

    between = jnp.where(even | (count_of(two) == 0), 0, tok)
    before_near = count_of(two) + count_of(odd)
    meta_near = meta_of(before_near + between)
    m, acc = forward(
        "attn_near", meta_near, query_rows, (two, odd), (WINDOW - 2 * tok, -8), (m, acc)
    )
    m, four, weight_t = lax.optimization_barrier((m, four, weight_t))
    rest = swap(jnp.where(even, kv, four), "core")
    meta = meta_of(before_near + count_of(four) + count_of(rest))

    weight_z = weight_t.reshape(n_z, 2, -1, weight_t.shape[1])

    def weight_for(steps):
        half = lax.dynamic_slice(
            weight_z, ((z + steps) % n_z, core, 0, 0), (1, 1) + weight_z.shape[2:]
        )
        return half[0, 0]

    fetched = [z_shift(weight_for(s), s) for s in range(1, n_z)]
    attn, lse = forward(
        "attn_far", meta, query_rows, (rest, four), (-9, WINDOW - 4 * tok), (m, acc), last=True
    )
    attns = [attn] + [z_shift(attn, s) for s in range(1, n_z)]

    dw = weight_grad_of(out_grad, attn)
    dw = lax.psum_scatter(dw, ("xl", "y"), scatter_dimension=0, tiled=True)
    dw = dw.reshape(2, -1, dw.shape[1])
    dw_mine = lax.dynamic_index_in_dim(dw, core, 0, keepdims=False)
    dw_other = swap(lax.dynamic_index_in_dim(dw, 1 - core, 0, keepdims=False), "core")
    weight_grad = lax.optimization_barrier(dw_mine.astype(F32) + dw_other.astype(F32)).T

    weight_d, _, fetched = lax.optimization_barrier((weight_t, attn, fetched))
    d_attn = d_attn_of(out_grad, weight_d)
    w_mine = jnp.concatenate([weight_for(0)] + fetched, 0)
    w_other = swap(w_mine, "core")

    common = (query_rows, d_attn, attn, lse)
    rest_part, four_part, dqt = backward(
        "attn_back_far", meta, common, (rest, four), (-9, WINDOW - 4 * tok)
    )
    rest_part, attns = lax.optimization_barrier((rest_part, attns))
    rest_part = [swap(rest_part[:, h : h + HEAD_DIM], "core") for h in (0, HEAD_DIM)]
    rest_part = jnp.concatenate(rest_part, 1).astype(F32)
    four_sum = (four_part.astype(F32) + jnp.where(even, 0.0, rest_part)).astype(BF16)
    out_other = out_part("out_other", jnp.stack([1 - xh, core]), attns, w_mine, w_other)
    dqt, four_sum, out_other = lax.optimization_barrier((dqt, four_sum, out_other))
    four_sum = ctx_shift(four_sum, -2)
    out_other = swap(out_other, "xh")

    odd_part, two_part, dqt = backward(
        "attn_back_mid", meta, common, (odd, two), (-8, WINDOW - 2 * tok), dqt
    )
    odd_part, four_sum = lax.optimization_barrier((odd_part, four_sum))
    odd_part = swap(odd_part, "core").astype(F32)
    two_sum = (two_part.astype(F32) + odd_part + four_sum.astype(F32)).astype(BF16)
    dqt, two_sum, out_other = lax.optimization_barrier((dqt, two_sum, out_other))
    two_sum = ctx_shift(two_sum, -2)

    own, query_grad = backward("attn_back_own", meta, common, (kv,), (WINDOW,), dqt, last=True)
    layer_out = out_part(
        "out_mine", jnp.stack([xh, core]), attns, w_mine, w_other, (out_other,)
    ).T

    own = own + jnp.where(even, rest_part, 0.0)
    own = (own + two_sum.astype(F32)).astype(BF16)
    return layer_out, query_grad, own[:, :HEAD_DIM], own[:, HEAD_DIM:], weight_grad


def solution(mesh):
    fine = Mesh(mesh.devices.reshape(2, 4, 2, 4, 2), CTX + FSDP)
    in_specs = (
        P(CTX, FSDP),
        P(CTX, FSDP),
        P(CTX, FSDP),
        P(CTX),
        P(FSDP, CTX),
        P(CTX, None),
    )
    out_specs = (
        P(CTX, FSDP),
        P(CTX, FSDP),
        P(CTX, FSDP),
        P(CTX, FSDP),
        P(FSDP, CTX),
    )
    return jax.shard_map(body, mesh=fine, in_specs=in_specs, out_specs=out_specs, check_vma=False)
```

```python
import functools
import math

import jax
import jax.numpy as jnp
from jax import lax
from jax.experimental import pallas as pl
from jax.experimental.pallas import tpu as pltpu
from jax.sharding import Mesh, PartitionSpec as P

HEAD_DIM = 128
WINDOW = 4096
N_DOCS = 4
SCALE = 1.0 / 12.0
SCALE2 = math.log2(math.e) / 12.0
NEG = -1e30
FAR = 1 << 30
F32 = jnp.float32
BF16 = jnp.bfloat16
NT = (((1,), (1,)), ((), ()))
NN = (((1,), (0,)), ((), ()))

TOK = 1024
BQ = 512
BK = 512
D_ROWS = 256
W_COLS = 1152

CTX = ("xl", "y", "core")
FSDP = ("z", "xh")


def first_seen(meta, i):
    low = i + 1
    for d in range(N_DOCS):
        low = jnp.maximum(low, jnp.where(i >= meta[d], meta[N_DOCS + d], 0))
    return low


def heads_of(ref, q0):
    rows = pl.ds(q0, BQ)
    return jnp.concatenate([ref[rows, 0:HEAD_DIM], ref[rows, HEAD_DIM : 2 * HEAD_DIM]], 0)


def masked_tile(meta, tile, q0, place):
    i = q0 + lax.broadcasted_iota(jnp.int32, (1, BQ), 1)
    low = first_seen(meta, i) - place
    high = WINDOW + i - place
    row = lax.broadcasted_iota(jnp.int32, (BK, BQ), 0)
    seen = (row >= low) & (row <= high)
    return jnp.concatenate(
        [jnp.where(seen, tile[:, :BQ], NEG), jnp.where(seen, tile[:, BQ:], NEG)], 1
    )


def for_tiles(meta, q0, base, rows, tile):
    low_first = first_seen(meta, q0)
    low_last = first_seen(meta, q0 + BQ - 1)
    begin = jnp.maximum(low_first - base, 0) // BK
    end = jnp.minimum((WINDOW + q0 + BQ - 1 - base) // BK + 1, rows // BK)

    def step(t, carry):
        row = pl.multiple_of((end - 1 - t) * BK, BK)
        place = base + row
        plain = (place >= low_last) & (place + BK - 1 <= WINDOW + q0)

        @pl.when(plain)
        def _():
            tile(row, place, False)

        @pl.when(jnp.logical_not(plain))
        def _():
            tile(row, place, True)

        return carry

    lax.fori_loop(0, end - begin, step, 0)


def for_queries(tok, work):
    def step(t, carry):
        work(pl.multiple_of(t * BQ, BQ), pl.multiple_of(t * 2 * BQ, 2 * BQ))
        return carry

    lax.fori_loop(0, tok // BQ, step, 0)


def forward_tile(meta, q2, q0, k_ref, v_ref, m_ref, acc_ref, row, place, masked):
    k = k_ref[pl.ds(row, BK), :]
    v = v_ref[pl.ds(row, BK), :]
    s = lax.dot_general(k, q2, NT, preferred_element_type=F32)
    if masked:
        s = masked_tile(meta, s, q0, place)
    m_old = m_ref[0:1, :]
    m_new = jnp.maximum(m_old, jnp.max(s, axis=0, keepdims=True))
    p = jnp.exp2((s - m_new) * SCALE2)
    shrink = jnp.exp2((m_old - m_new) * SCALE2)
    v_ones = jnp.concatenate([v.T, jnp.ones((16, BK), BF16)], 0)
    acc_ref[...] = acc_ref[...] * shrink + lax.dot_general(
        v_ones, p.astype(BF16), NN, preferred_element_type=F32
    )
    m_ref[...] = jnp.broadcast_to(m_new, m_ref.shape)


def key_part(ref):
    return ref.at[:, 0:HEAD_DIM]


def value_part(ref):
    return ref.at[:, HEAD_DIM : 2 * HEAD_DIM]


def base_of(meta, base):
    return base if base >= 0 else meta[-base]


def forward_kernel(bases, first, last, meta, q_ref, *refs):
    n = len(bases)
    block_refs, refs = refs[:n], refs[n:]
    if not first:
        (m_in, acc_in), refs = refs[:2], refs[2:]
    one_out, two_out, m_ref, acc_ref = refs

    def work(q0, c0):
        cols = pl.ds(c0, 2 * BQ)
        q2 = heads_of(q_ref, q0)
        m_ref[...] = jnp.full(m_ref.shape, NEG, F32) if first else m_in[:, cols]
        acc_ref[...] = jnp.zeros(acc_ref.shape, F32) if first else acc_in[:, cols]
        for ref, base in zip(block_refs, bases):
            tile = functools.partial(
                forward_tile, meta, q2, q0, key_part(ref), value_part(ref), m_ref, acc_ref
            )
            for_tiles(meta, q0, base_of(meta, base), TOK, tile)
        if last:
            o = (acc_ref[0:HEAD_DIM, :] / acc_ref[HEAD_DIM : HEAD_DIM + 1, :]).T
            one_out[pl.ds(q0, BQ), 0:HEAD_DIM] = o[:BQ].astype(BF16)
            one_out[pl.ds(q0, BQ), HEAD_DIM : 2 * HEAD_DIM] = o[BQ:].astype(BF16)
            two_out[:, cols] = m_ref[...] * SCALE2 + jnp.log2(acc_ref[HEAD_DIM : HEAD_DIM + 8, :])
        else:
            one_out[:, cols] = m_ref[...]
            two_out[:, cols] = acc_ref[...]

    for_queries(TOK, work)


def forward(name, meta, q, blocks, bases, state=(), last=False):
    out = (
        jax.ShapeDtypeStruct((8, 2 * TOK), F32),
        jax.ShapeDtypeStruct((HEAD_DIM + 16, 2 * TOK), F32),
    )
    if last:
        out = (jax.ShapeDtypeStruct((TOK, 2 * HEAD_DIM), BF16), out[0])
    scratch = [pltpu.VMEM((8, 2 * BQ), F32), pltpu.VMEM((HEAD_DIM + 16, 2 * BQ), F32)]
    args = [q] + list(blocks) + list(state)
    kernel = functools.partial(forward_kernel, bases, not state, last)
    return call(kernel, name, len(args), out, scratch, 20)(meta, *args)


def call(kernel, name, n_vmem, out_shape, scratch, vmem_mb, cost=0):
    vmem = pl.BlockSpec(memory_space=pltpu.VMEM)
    return pl.pallas_call(
        kernel,
        out_shape=out_shape,
        in_specs=[pl.BlockSpec(memory_space=pltpu.SMEM)] + [vmem] * n_vmem,
        out_specs=jax.tree.map(lambda _: vmem, out_shape),
        scratch_shapes=scratch,
        compiler_params=pltpu.CompilerParams(vmem_limit_bytes=vmem_mb * 2**20),
        cost_estimate=pl.CostEstimate(flops=cost, bytes_accessed=0, transcendentals=0),
        name=name,
    )


def backward_kernel(bases, first, last, meta, q_ref, do_ref, o_ref, lse_ref, *refs):
    tok = q_ref.shape[0]
    n = len(bases)
    block_refs, refs = refs[:n], refs[n:]
    if not first:
        dqt_in, refs = refs[0], refs[1:]
    part_refs, dq_ref, (dqt, dk, dv) = refs[:n], refs[n], refs[n + 1 :]
    dk[...] = jnp.zeros(dk.shape, F32)
    dv[...] = jnp.zeros(dv.shape, F32)

    def work(q0, c0):
        cols = pl.ds(c0, 2 * BQ)
        q2 = heads_of(q_ref, q0)
        do2 = heads_of(do_ref, q0)
        o2 = heads_of(o_ref, q0)
        delta = jnp.sum((do2.astype(F32) * o2.astype(F32)).T, axis=0, keepdims=True)
        lse = lse_ref[0:1, cols]
        dqt[...] = jnp.zeros(dqt.shape, F32) if first else dqt_in[:, cols]

        def tile(index, row, place, masked):
            ref = block_refs[index]
            k = ref[pl.ds(row, BK), 0:HEAD_DIM]
            v = ref[pl.ds(row, BK), HEAD_DIM : 2 * HEAD_DIM]
            t = lax.dot_general(k, q2, NT, preferred_element_type=F32) * SCALE2 - lse
            if masked:
                t = masked_tile(meta, t, q0, place)
            p = jnp.exp2(t)
            dp = lax.dot_general(v, do2, NT, preferred_element_type=F32)
            ds = (p * (dp - delta)).astype(BF16)
            rows = pl.ds(row, BK)
            dv[index, rows, :] += lax.dot_general(
                p.astype(BF16), do2, NN, preferred_element_type=F32
            )
            dk[index, rows, :] += lax.dot_general(ds, q2, NN, preferred_element_type=F32)
            dqt[...] += lax.dot_general(k.T, ds, NN, preferred_element_type=F32)

        for index, base in enumerate(bases):
            for_tiles(meta, q0, base_of(meta, base), tok, functools.partial(tile, index))
        if last:
            dq = (dqt[...] * SCALE).T
            dq_ref[pl.ds(q0, BQ), 0:HEAD_DIM] = dq[:BQ].astype(BF16)
            dq_ref[pl.ds(q0, BQ), HEAD_DIM : 2 * HEAD_DIM] = dq[BQ:].astype(BF16)
        else:
            dq_ref[:, cols] = dqt[...]

    for_queries(tok, work)
    for index, ref in enumerate(part_refs):
        ref[:, 0:HEAD_DIM] = (dk[index] * SCALE).astype(ref.dtype)
        ref[:, HEAD_DIM : 2 * HEAD_DIM] = dv[index].astype(ref.dtype)


def backward(name, meta, common, blocks, bases, dqt=None, last=False):
    tok = common[0].shape[0]
    n = len(blocks)
    part = jax.ShapeDtypeStruct((tok, 2 * HEAD_DIM), F32 if last else BF16)
    dq = ((tok, 2 * HEAD_DIM), BF16) if last else ((HEAD_DIM, 2 * tok), F32)
    scratch = [
        pltpu.VMEM((HEAD_DIM, 2 * BQ), F32),
        pltpu.VMEM((n, tok, HEAD_DIM), F32),
        pltpu.VMEM((n, tok, HEAD_DIM), F32),
    ]
    args = list(common) + list(blocks) + ([] if dqt is None else [dqt])
    kernel = functools.partial(backward_kernel, bases, dqt is None, last)
    out = (part,) * n + (jax.ShapeDtypeStruct(*dq),)
    cost = 0 if dqt is None or last else 20_000_000_000
    return call(kernel, name, len(args), out, scratch, 30, cost)(meta, *args)


def d_attn_kernel(og_ref, wt_ref, out_ref):
    out_ref[...] = lax.dot_general(
        og_ref[...], wt_ref[...], NN, preferred_element_type=F32
    ).astype(BF16)


def weight_grad_kernel(og_ref, attn_ref, out_ref, attn_t):
    @pl.when(pl.program_id(0) == 0)
    def _():
        attn_t[...] = attn_ref[...].T

    out_ref[...] = lax.dot_general(
        attn_t[...], og_ref[...], NN, preferred_element_type=F32
    ).T.astype(BF16)


def streamed(kernel, name, steps, in_specs, out_spec, out_shape, scratch):
    return pl.pallas_call(
        kernel,
        grid=(steps,),
        out_shape=out_shape,
        in_specs=in_specs,
        out_specs=out_spec,
        scratch_shapes=scratch,
        compiler_params=pltpu.CompilerParams(vmem_limit_bytes=58 * 2**20),
        cost_estimate=pl.CostEstimate(flops=0, bytes_accessed=0, transcendentals=0),
        name=name,
    )


def d_attn_of(out_grad, weight_t):
    tok, width = out_grad.shape
    heads = weight_t.shape[1]
    in_specs = [
        pl.BlockSpec((D_ROWS, width), lambda i: (i, 0)),
        pl.BlockSpec((width, heads), lambda i: (0, 0)),
    ]
    out_spec = pl.BlockSpec((D_ROWS, heads), lambda i: (i, 0))
    out = jax.ShapeDtypeStruct((tok, heads), BF16)
    return streamed(d_attn_kernel, "d_attn", tok // D_ROWS, in_specs, out_spec, out, [])(
        out_grad, weight_t
    )


def weight_grad_of(out_grad, attn):
    tok, width = out_grad.shape
    heads = attn.shape[1]
    in_specs = [
        pl.BlockSpec((tok, W_COLS), lambda i: (0, i)),
        pl.BlockSpec((tok, heads), lambda i: (0, 0)),
    ]
    out_spec = pl.BlockSpec((W_COLS, heads), lambda i: (i, 0))
    out = jax.ShapeDtypeStruct((width, heads), BF16)
    scratch = [pltpu.VMEM((heads, tok), BF16)]
    return streamed(
        weight_grad_kernel, "weight_grad", width // W_COLS, in_specs, out_spec, out, scratch
    )(out_grad, attn)


def out_kernel(n, where, mine_ref, other_ref, *refs):
    attn_refs, refs = refs[:n], refs[n:]
    out_ref = refs[-1]
    cols = out_ref.shape[0]

    def with_weights(w_ref):
        total = refs[0][...].astype(F32) if len(refs) == 2 else None
        for i, a_ref in enumerate(attn_refs):
            w = w_ref[i * cols : (i + 1) * cols, :]
            term = lax.dot_general(w, a_ref[...], NT, preferred_element_type=F32)
            total = term if total is None else total + term
        out_ref[...] = total.astype(BF16)

    @pl.when(where[0] == where[1])
    def _():
        with_weights(mine_ref)

    @pl.when(where[0] != where[1])
    def _():
        with_weights(other_ref)


def out_part(name, where, attns, mine, other, extra=()):
    args = [mine, other] + list(attns) + list(extra)
    out = jax.ShapeDtypeStruct((mine.shape[0] // len(attns), TOK), BF16)
    kernel = functools.partial(out_kernel, len(attns))
    return call(kernel, name, len(args), out, [], 20)(where, *args)


def ctx_shift(value, steps):
    count = lax.axis_size(CTX)
    leading, last = max(0, -steps), min(count, count - steps)
    return lax.ppermute(value, CTX, [(s, s + steps) for s in range(leading, last)])


def swap(value, axis):
    return lax.ppermute(value, axis, [(0, 1), (1, 0)])


def z_shift(value, steps):
    count = lax.axis_size("z")
    return lax.ppermute(value, "z", [(s, (s + steps) % count) for s in range(count)])


def body(query_rows, key_rows, value_rows, doc_ids, out_weight, out_grad):
    tok = query_rows.shape[0]
    core = lax.axis_index("core")
    even = core == 0
    z = lax.axis_index("z")
    xh = lax.axis_index("xh")
    n_z = lax.axis_size("z")

    weight_t = lax.all_gather(out_weight.T, CTX, axis=0, tiled=True)

    docs = lax.iota(jnp.int32, N_DOCS)
    count = jnp.sum((doc_ids[None, :] == docs[:, None]).astype(jnp.int32), axis=1)
    info = jnp.stack([count // 32, count % 32]).astype(BF16)
    info = jnp.pad(info, ((0, 14), (0, 2 * HEAD_DIM - N_DOCS)))
    kv = jnp.concatenate([jnp.concatenate([key_rows, value_rows], 1), info], 0)
    two = ctx_shift(kv, 2)

    def count_of(block):
        high, low = block[tok, :N_DOCS], block[tok + 1, :N_DOCS]
        return (high.astype(F32) * 32 + low.astype(F32)).astype(jnp.int32)

    local_start = jnp.cumsum(count) - count
    present = count > 0
    odd_base = jnp.where(even, WINDOW - tok, WINDOW - 3 * tok)
    rest_base = jnp.where(even, WINDOW - 3 * tok, WINDOW - tok)

    def meta_of(before):
        return jnp.concatenate(
            [
                jnp.where(present, local_start, FAR),
                jnp.where(present, WINDOW + local_start - before, 0),
                jnp.stack([odd_base, rest_base]).astype(jnp.int32),
            ]
        )

    meta_own = meta_of(jnp.zeros_like(count))
    m, acc = forward("attn_own", meta_own, query_rows, (kv,), (WINDOW,))
    m, two = lax.optimization_barrier((m, two))
    odd = swap(two, "core")
    four = ctx_shift(two, 2)

    between = jnp.where(even | (count_of(two) == 0), 0, tok)
    before_near = count_of(two) + count_of(odd)
    meta_near = meta_of(before_near + between)
    m, acc = forward(
        "attn_near", meta_near, query_rows, (two, odd), (WINDOW - 2 * tok, -8), (m, acc)
    )
    m, four, weight_t = lax.optimization_barrier((m, four, weight_t))
    rest = swap(jnp.where(even, kv, four), "core")
    meta = meta_of(before_near + count_of(four) + count_of(rest))

    weight_z = weight_t.reshape(n_z, 2, -1, weight_t.shape[1])

    def weight_for(steps):
        half = lax.dynamic_slice(
            weight_z, ((z + steps) % n_z, core, 0, 0), (1, 1) + weight_z.shape[2:]
        )
        return half[0, 0]

    fetched = [z_shift(weight_for(s), s) for s in range(1, n_z)]
    attn, lse = forward(
        "attn_far", meta, query_rows, (rest, four), (-9, WINDOW - 4 * tok), (m, acc), last=True
    )
    attns = [attn] + [z_shift(attn, s) for s in range(1, n_z)]

    dw = weight_grad_of(out_grad, attn)
    dw = lax.psum_scatter(dw, ("xl", "y"), scatter_dimension=0, tiled=True)
    dw = dw.reshape(2, -1, dw.shape[1])
    dw_mine = lax.dynamic_index_in_dim(dw, core, 0, keepdims=False)
    dw_other = swap(lax.dynamic_index_in_dim(dw, 1 - core, 0, keepdims=False), "core")
    weight_grad = lax.optimization_barrier(dw_mine.astype(F32) + dw_other.astype(F32)).T

    weight_d, _, fetched = lax.optimization_barrier((weight_t, attn, fetched))
    d_attn = d_attn_of(out_grad, weight_d)
    w_mine = jnp.concatenate([weight_for(0)] + fetched, 0)
    w_other = swap(w_mine, "core")

    common = (query_rows, d_attn, attn, lse)
    rest_part, four_part, dqt = backward(
        "attn_back_far", meta, common, (rest, four), (-9, WINDOW - 4 * tok)
    )
    rest_part, attns = lax.optimization_barrier((rest_part, attns))
    rest_part = [swap(rest_part[:, h : h + HEAD_DIM], "core") for h in (0, HEAD_DIM)]
    rest_part = jnp.concatenate(rest_part, 1).astype(F32)
    four_sum = (four_part.astype(F32) + jnp.where(even, 0.0, rest_part)).astype(BF16)
    out_other = out_part("out_other", jnp.stack([1 - xh, core]), attns, w_mine, w_other)
    dqt, four_sum, out_other = lax.optimization_barrier((dqt, four_sum, out_other))
    four_sum = ctx_shift(four_sum, -2)
    out_other = swap(out_other, "xh")

    odd_part, two_part, dqt = backward(
        "attn_back_mid", meta, common, (odd, two), (-8, WINDOW - 2 * tok), dqt
    )
    odd_part, four_sum = lax.optimization_barrier((odd_part, four_sum))
    odd_part = swap(odd_part, "core").astype(F32)
    two_sum = (two_part.astype(F32) + odd_part + four_sum.astype(F32)).astype(BF16)
    dqt, two_sum = lax.optimization_barrier((dqt, two_sum))
    two_sum = ctx_shift(two_sum, -2)

    own, query_grad = backward("attn_back_own", meta, common, (kv,), (WINDOW,), dqt, last=True)
    layer_out = out_part(
        "out_mine", jnp.stack([xh, core]), attns, w_mine, w_other, (out_other,)
    ).T

    own = own + jnp.where(even, rest_part, 0.0)
    own = (own + two_sum.astype(F32)).astype(BF16)
    return layer_out, query_grad, own[:, :HEAD_DIM], own[:, HEAD_DIM:], weight_grad


def solution(mesh):
    fine = Mesh(mesh.devices.reshape(2, 4, 2, 4, 2), CTX + FSDP)
    in_specs = (
        P(CTX, FSDP),
        P(CTX, FSDP),
        P(CTX, FSDP),
        P(CTX),
        P(FSDP, CTX),
        P(CTX, None),
    )
    out_specs = (
        P(CTX, FSDP),
        P(CTX, FSDP),
        P(CTX, FSDP),
        P(CTX, FSDP),
        P(FSDP, CTX),
    )
    return jax.shard_map(body, mesh=fine, in_specs=in_specs, out_specs=out_specs, check_vma=False)
```

```python
import functools
import math

import jax
import jax.numpy as jnp
from jax import lax
from jax.experimental import pallas as pl
from jax.experimental.pallas import tpu as pltpu
from jax.sharding import Mesh, PartitionSpec as P

HEAD_DIM = 128
WINDOW = 4096
N_DOCS = 4
SCALE = 1.0 / 12.0
SCALE2 = math.log2(math.e) / 12.0
NEG = -1e30
FAR = 1 << 30
F32 = jnp.float32
BF16 = jnp.bfloat16
NT = (((1,), (1,)), ((), ()))
NN = (((1,), (0,)), ((), ()))

TOK = 1024
BQ = 512
BK = 512
D_ROWS = 256
W_COLS = 1152

CTX = ("xl", "y", "core")
FSDP = ("z", "xh")


def first_seen(meta, i):
    low = i + 1
    for d in range(N_DOCS):
        low = jnp.maximum(low, jnp.where(i >= meta[d], meta[N_DOCS + d], 0))
    return low


def heads_of(ref, q0):
    rows = pl.ds(q0, BQ)
    return jnp.concatenate([ref[rows, 0:HEAD_DIM], ref[rows, HEAD_DIM : 2 * HEAD_DIM]], 0)


def masked_tile(meta, tile, q0, place):
    i = q0 + lax.broadcasted_iota(jnp.int32, (1, BQ), 1)
    low = first_seen(meta, i) - place
    high = WINDOW + i - place
    row = lax.broadcasted_iota(jnp.int32, (BK, BQ), 0)
    seen = (row >= low) & (row <= high)
    return jnp.concatenate(
        [jnp.where(seen, tile[:, :BQ], NEG), jnp.where(seen, tile[:, BQ:], NEG)], 1
    )


def for_tiles(meta, q0, base, rows, tile):
    low_first = first_seen(meta, q0)
    low_last = first_seen(meta, q0 + BQ - 1)
    begin = jnp.maximum(low_first - base, 0) // BK
    end = jnp.minimum((WINDOW + q0 + BQ - 1 - base) // BK + 1, rows // BK)

    def step(t, carry):
        row = pl.multiple_of((end - 1 - t) * BK, BK)
        place = base + row
        plain = (place >= low_last) & (place + BK - 1 <= WINDOW + q0)

        @pl.when(plain)
        def _():
            tile(row, place, False)

        @pl.when(jnp.logical_not(plain))
        def _():
            tile(row, place, True)

        return carry

    lax.fori_loop(0, end - begin, step, 0)


def for_queries(tok, work):
    def step(t, carry):
        work(pl.multiple_of(t * BQ, BQ), pl.multiple_of(t * 2 * BQ, 2 * BQ))
        return carry

    lax.fori_loop(0, tok // BQ, step, 0)


def forward_tile(meta, q2, q0, k_ref, v_ref, m_ref, acc_ref, row, place, masked):
    k = k_ref[pl.ds(row, BK), :]
    v = v_ref[pl.ds(row, BK), :]
    s = lax.dot_general(k, q2, NT, preferred_element_type=F32)
    if masked:
        s = masked_tile(meta, s, q0, place)
    m_old = m_ref[0:1, :]
    m_new = jnp.maximum(m_old, jnp.max(s, axis=0, keepdims=True))
    p = jnp.exp2((s - m_new) * SCALE2)
    shrink = jnp.exp2((m_old - m_new) * SCALE2)
    v_ones = jnp.concatenate([v.T, jnp.ones((16, BK), BF16)], 0)
    acc_ref[...] = acc_ref[...] * shrink + lax.dot_general(
        v_ones, p.astype(BF16), NN, preferred_element_type=F32
    )
    m_ref[...] = jnp.broadcast_to(m_new, m_ref.shape)


def key_part(ref):
    return ref.at[:, 0:HEAD_DIM]


def value_part(ref):
    return ref.at[:, HEAD_DIM : 2 * HEAD_DIM]


def base_of(meta, base):
    return base if base >= 0 else meta[-base]


def forward_kernel(bases, first, last, meta, q_ref, *refs):
    n = len(bases)
    block_refs, refs = refs[:n], refs[n:]
    if not first:
        (m_in, acc_in), refs = refs[:2], refs[2:]
    one_out, two_out, m_ref, acc_ref = refs

    def work(q0, c0):
        cols = pl.ds(c0, 2 * BQ)
        q2 = heads_of(q_ref, q0)
        m_ref[...] = jnp.full(m_ref.shape, NEG, F32) if first else m_in[:, cols]
        acc_ref[...] = jnp.zeros(acc_ref.shape, F32) if first else acc_in[:, cols]
        for ref, base in zip(block_refs, bases):
            tile = functools.partial(
                forward_tile, meta, q2, q0, key_part(ref), value_part(ref), m_ref, acc_ref
            )
            for_tiles(meta, q0, base_of(meta, base), TOK, tile)
        if last:
            o = (acc_ref[0:HEAD_DIM, :] / acc_ref[HEAD_DIM : HEAD_DIM + 1, :]).T
            one_out[pl.ds(q0, BQ), 0:HEAD_DIM] = o[:BQ].astype(BF16)
            one_out[pl.ds(q0, BQ), HEAD_DIM : 2 * HEAD_DIM] = o[BQ:].astype(BF16)
            two_out[:, cols] = m_ref[...] * SCALE2 + jnp.log2(acc_ref[HEAD_DIM : HEAD_DIM + 8, :])
        else:
            one_out[:, cols] = m_ref[...]
            two_out[:, cols] = acc_ref[...]

    for_queries(TOK, work)


def forward(name, meta, q, blocks, bases, state=(), last=False):
    out = (
        jax.ShapeDtypeStruct((8, 2 * TOK), F32),
        jax.ShapeDtypeStruct((HEAD_DIM + 16, 2 * TOK), F32),
    )
    if last:
        out = (jax.ShapeDtypeStruct((TOK, 2 * HEAD_DIM), BF16), out[0])
    scratch = [pltpu.VMEM((8, 2 * BQ), F32), pltpu.VMEM((HEAD_DIM + 16, 2 * BQ), F32)]
    args = [q] + list(blocks) + list(state)
    kernel = functools.partial(forward_kernel, bases, not state, last)
    return call(kernel, name, len(args), out, scratch, 20)(meta, *args)


def call(kernel, name, n_vmem, out_shape, scratch, vmem_mb, cost=0):
    vmem = pl.BlockSpec(memory_space=pltpu.VMEM)
    return pl.pallas_call(
        kernel,
        out_shape=out_shape,
        in_specs=[pl.BlockSpec(memory_space=pltpu.SMEM)] + [vmem] * n_vmem,
        out_specs=jax.tree.map(lambda _: vmem, out_shape),
        scratch_shapes=scratch,
        compiler_params=pltpu.CompilerParams(vmem_limit_bytes=vmem_mb * 2**20),
        cost_estimate=pl.CostEstimate(flops=cost, bytes_accessed=0, transcendentals=0),
        name=name,
    )


def backward_kernel(bases, first, last, meta, q_ref, do_ref, o_ref, lse_ref, *refs):
    tok = q_ref.shape[0]
    n = len(bases)
    block_refs, refs = refs[:n], refs[n:]
    if not first:
        dqt_in, refs = refs[0], refs[1:]
    part_refs, dq_ref, (dqt, dk, dv) = refs[:n], refs[n], refs[n + 1 :]
    dk[...] = jnp.zeros(dk.shape, F32)
    dv[...] = jnp.zeros(dv.shape, F32)

    def work(q0, c0):
        cols = pl.ds(c0, 2 * BQ)
        q2 = heads_of(q_ref, q0)
        do2 = heads_of(do_ref, q0)
        o2 = heads_of(o_ref, q0)
        delta = jnp.sum((do2.astype(F32) * o2.astype(F32)).T, axis=0, keepdims=True)
        lse = lse_ref[0:1, cols]
        dqt[...] = jnp.zeros(dqt.shape, F32) if first else dqt_in[:, cols]

        def tile(index, row, place, masked):
            ref = block_refs[index]
            k = ref[pl.ds(row, BK), 0:HEAD_DIM]
            v = ref[pl.ds(row, BK), HEAD_DIM : 2 * HEAD_DIM]
            t = lax.dot_general(k, q2, NT, preferred_element_type=F32) * SCALE2 - lse
            if masked:
                t = masked_tile(meta, t, q0, place)
            p = jnp.exp2(t)
            dp = lax.dot_general(v, do2, NT, preferred_element_type=F32)
            ds = (p * (dp - delta)).astype(BF16)
            rows = pl.ds(row, BK)
            dv[index, rows, :] += lax.dot_general(
                p.astype(BF16), do2, NN, preferred_element_type=F32
            )
            dk[index, rows, :] += lax.dot_general(ds, q2, NN, preferred_element_type=F32)
            dqt[...] += lax.dot_general(k.T, ds, NN, preferred_element_type=F32)

        for index, base in enumerate(bases):
            for_tiles(meta, q0, base_of(meta, base), tok, functools.partial(tile, index))
        if last:
            dq = (dqt[...] * SCALE).T
            dq_ref[pl.ds(q0, BQ), 0:HEAD_DIM] = dq[:BQ].astype(BF16)
            dq_ref[pl.ds(q0, BQ), HEAD_DIM : 2 * HEAD_DIM] = dq[BQ:].astype(BF16)
        else:
            dq_ref[:, cols] = dqt[...]

    for_queries(tok, work)
    for index, ref in enumerate(part_refs):
        ref[:, 0:HEAD_DIM] = (dk[index] * SCALE).astype(ref.dtype)
        ref[:, HEAD_DIM : 2 * HEAD_DIM] = dv[index].astype(ref.dtype)


def backward(name, meta, common, blocks, bases, dqt=None, last=False):
    tok = common[0].shape[0]
    n = len(blocks)
    part = jax.ShapeDtypeStruct((tok, 2 * HEAD_DIM), F32 if last else BF16)
    dq = ((tok, 2 * HEAD_DIM), BF16) if last else ((HEAD_DIM, 2 * tok), F32)
    scratch = [
        pltpu.VMEM((HEAD_DIM, 2 * BQ), F32),
        pltpu.VMEM((n, tok, HEAD_DIM), F32),
        pltpu.VMEM((n, tok, HEAD_DIM), F32),
    ]
    args = list(common) + list(blocks) + ([] if dqt is None else [dqt])
    kernel = functools.partial(backward_kernel, bases, dqt is None, last)
    out = (part,) * n + (jax.ShapeDtypeStruct(*dq),)
    cost = 0 if dqt is None or last else 20_000_000_000
    return call(kernel, name, len(args), out, scratch, 30, cost)(meta, *args)


def d_attn_kernel(og_ref, wt_ref, out_ref):
    out_ref[...] = lax.dot_general(
        og_ref[...], wt_ref[...], NN, preferred_element_type=F32
    ).astype(BF16)


def weight_grad_kernel(og_ref, attn_ref, out_ref, attn_t):
    @pl.when(pl.program_id(0) == 0)
    def _():
        attn_t[...] = attn_ref[...].T

    out_ref[...] = lax.dot_general(
        attn_t[...], og_ref[...], NN, preferred_element_type=F32
    ).T.astype(BF16)


def streamed(kernel, name, steps, in_specs, out_spec, out_shape, scratch):
    return pl.pallas_call(
        kernel,
        grid=(steps,),
        out_shape=out_shape,
        in_specs=in_specs,
        out_specs=out_spec,
        scratch_shapes=scratch,
        compiler_params=pltpu.CompilerParams(vmem_limit_bytes=58 * 2**20),
        cost_estimate=pl.CostEstimate(flops=0, bytes_accessed=0, transcendentals=0),
        name=name,
    )


def d_attn_of(out_grad, weight_t):
    tok, width = out_grad.shape
    heads = weight_t.shape[1]
    in_specs = [
        pl.BlockSpec((D_ROWS, width), lambda i: (i, 0)),
        pl.BlockSpec((width, heads), lambda i: (0, 0)),
    ]
    out_spec = pl.BlockSpec((D_ROWS, heads), lambda i: (i, 0))
    out = jax.ShapeDtypeStruct((tok, heads), BF16)
    return streamed(d_attn_kernel, "d_attn", tok // D_ROWS, in_specs, out_spec, out, [])(
        out_grad, weight_t
    )


def weight_grad_of(out_grad, attn):
    tok, width = out_grad.shape
    heads = attn.shape[1]
    in_specs = [
        pl.BlockSpec((tok, W_COLS), lambda i: (0, i)),
        pl.BlockSpec((tok, heads), lambda i: (0, 0)),
    ]
    out_spec = pl.BlockSpec((W_COLS, heads), lambda i: (i, 0))
    out = jax.ShapeDtypeStruct((width, heads), BF16)
    scratch = [pltpu.VMEM((heads, tok), BF16)]
    return streamed(
        weight_grad_kernel, "weight_grad", width // W_COLS, in_specs, out_spec, out, scratch
    )(out_grad, attn)


def out_kernel(n, where, mine_ref, other_ref, *refs):
    attn_refs, refs = refs[:n], refs[n:]
    out_ref = refs[-1]
    cols = out_ref.shape[0]

    def with_weights(w_ref):
        total = refs[0][...].astype(F32) if len(refs) == 2 else None
        for i, a_ref in enumerate(attn_refs):
            w = w_ref[i * cols : (i + 1) * cols, :]
            term = lax.dot_general(w, a_ref[...], NT, preferred_element_type=F32)
            total = term if total is None else total + term
        out_ref[...] = total.astype(BF16)

    @pl.when(where[0] == where[1])
    def _():
        with_weights(mine_ref)

    @pl.when(where[0] != where[1])
    def _():
        with_weights(other_ref)


def out_part(name, where, attns, mine, other, extra=()):
    args = [mine, other] + list(attns) + list(extra)
    out = jax.ShapeDtypeStruct((mine.shape[0] // len(attns), TOK), BF16)
    kernel = functools.partial(out_kernel, len(attns))
    return call(kernel, name, len(args), out, [], 20)(where, *args)


def ctx_shift(value, steps):
    count = lax.axis_size(CTX)
    leading, last = max(0, -steps), min(count, count - steps)
    return lax.ppermute(value, CTX, [(s, s + steps) for s in range(leading, last)])


def swap(value, axis):
    return lax.ppermute(value, axis, [(0, 1), (1, 0)])


def z_shift(value, steps):
    count = lax.axis_size("z")
    return lax.ppermute(value, "z", [(s, (s + steps) % count) for s in range(count)])


def body(query_rows, key_rows, value_rows, doc_ids, out_weight, out_grad):
    tok = query_rows.shape[0]
    core = lax.axis_index("core")
    even = core == 0
    z = lax.axis_index("z")
    xh = lax.axis_index("xh")
    n_z = lax.axis_size("z")

    weight_t = lax.all_gather(out_weight.T, CTX, axis=0, tiled=True)

    docs = lax.iota(jnp.int32, N_DOCS)
    count = jnp.sum((doc_ids[None, :] == docs[:, None]).astype(jnp.int32), axis=1)
    info = jnp.stack([count // 32, count % 32]).astype(BF16)
    info = jnp.pad(info, ((0, 14), (0, 2 * HEAD_DIM - N_DOCS)))
    kv = jnp.concatenate([jnp.concatenate([key_rows, value_rows], 1), info], 0)
    two = ctx_shift(kv, 2)

    def count_of(block):
        high, low = block[tok, :N_DOCS], block[tok + 1, :N_DOCS]
        return (high.astype(F32) * 32 + low.astype(F32)).astype(jnp.int32)

    local_start = jnp.cumsum(count) - count
    present = count > 0
    odd_base = jnp.where(even, WINDOW - tok, WINDOW - 3 * tok)
    rest_base = jnp.where(even, WINDOW - 3 * tok, WINDOW - tok)

    def meta_of(before):
        return jnp.concatenate(
            [
                jnp.where(present, local_start, FAR),
                jnp.where(present, WINDOW + local_start - before, 0),
                jnp.stack([odd_base, rest_base]).astype(jnp.int32),
            ]
        )

    meta_own = meta_of(jnp.zeros_like(count))
    m, acc = forward("attn_own", meta_own, query_rows, (kv,), (WINDOW,))
    m, two = lax.optimization_barrier((m, two))
    odd = swap(two, "core")
    four = ctx_shift(two, 2)

    between = jnp.where(even | (count_of(two) == 0), 0, tok)
    before_near = count_of(two) + count_of(odd)
    meta_near = meta_of(before_near + between)
    m, acc = forward(
        "attn_near", meta_near, query_rows, (two, odd), (WINDOW - 2 * tok, -8), (m, acc)
    )
    m, four, weight_t = lax.optimization_barrier((m, four, weight_t))
    rest = swap(jnp.where(even, kv, four), "core")
    meta = meta_of(before_near + count_of(four) + count_of(rest))

    weight_z = weight_t.reshape(n_z, 2, -1, weight_t.shape[1])

    def weight_for(steps):
        half = lax.dynamic_slice(
            weight_z, ((z + steps) % n_z, core, 0, 0), (1, 1) + weight_z.shape[2:]
        )
        return half[0, 0]

    fetched = [z_shift(weight_for(s), s) for s in range(1, n_z)]
    attn, lse = forward(
        "attn_far", meta, query_rows, (rest, four), (-9, WINDOW - 4 * tok), (m, acc), last=True
    )
    attns = [attn] + [z_shift(attn, s) for s in range(1, n_z)]

    dw = weight_grad_of(out_grad, attn)
    dw = lax.psum_scatter(dw, ("xl", "y"), scatter_dimension=0, tiled=True)
    dw = dw.reshape(2, -1, dw.shape[1])
    dw_mine = lax.dynamic_index_in_dim(dw, core, 0, keepdims=False)
    dw_other = swap(lax.dynamic_index_in_dim(dw, 1 - core, 0, keepdims=False), "core")
    weight_grad = lax.optimization_barrier(dw_mine.astype(F32) + dw_other.astype(F32)).T

    weight_d, _, fetched = lax.optimization_barrier((weight_t, attn, fetched))
    d_attn = d_attn_of(out_grad, weight_d)
    w_mine = jnp.concatenate([weight_for(0)] + fetched, 0)
    w_other = swap(w_mine, "core")

    common = (query_rows, d_attn, attn, lse)
    rest_part, four_part, dqt = backward(
        "attn_back_far", meta, common, (rest, four), (-9, WINDOW - 4 * tok)
    )
    rest_part, attns = lax.optimization_barrier((rest_part, attns))
    rest_part = [swap(rest_part[:, h : h + HEAD_DIM], "core") for h in (0, HEAD_DIM)]
    rest_part = jnp.concatenate(rest_part, 1).astype(F32)
    four_sum = (four_part.astype(F32) + jnp.where(even, 0.0, rest_part)).astype(BF16)
    out_other = out_part("out_other", jnp.stack([1 - xh, core]), attns, w_mine, w_other)
    dqt, four_sum, out_other = lax.optimization_barrier((dqt, four_sum, out_other))
    four_sum = ctx_shift(four_sum, -2)
    out_other = swap(out_other, "xh")

    odd_part, two_part, dqt = backward(
        "attn_back_mid", meta, common, (odd, two), (-8, WINDOW - 2 * tok), dqt
    )
    odd_part, four_sum = lax.optimization_barrier((odd_part, four_sum))
    odd_part = swap(odd_part, "core").astype(F32)
    two_sum = (two_part.astype(F32) + odd_part + four_sum.astype(F32)).astype(BF16)
    dqt, two_sum, out_other = lax.optimization_barrier((dqt, two_sum, out_other))
    two_sum = ctx_shift(two_sum, -2)

    own, query_grad = backward("attn_back_own", meta, common, (kv,), (WINDOW,), dqt, last=True)
    layer_out = out_part(
        "out_mine", jnp.stack([xh, core]), attns, w_mine, w_other, (out_other,)
    ).T

    own = own + jnp.where(even, rest_part, 0.0)
    own = (own + two_sum.astype(F32)).astype(BF16)
    return layer_out, query_grad, own[:, :HEAD_DIM], own[:, HEAD_DIM:], weight_grad


def solution(mesh):
    fine = Mesh(mesh.devices.reshape(2, 4, 2, 4, 2), CTX + FSDP)
    in_specs = (
        P(CTX, FSDP),
        P(CTX, FSDP),
        P(CTX, FSDP),
        P(CTX),
        P(FSDP, CTX),
        P(CTX, None),
    )
    out_specs = (
        P(CTX, FSDP),
        P(CTX, FSDP),
        P(CTX, FSDP),
        P(CTX, FSDP),
        P(FSDP, CTX),
    )
    return jax.shard_map(body, mesh=fine, in_specs=in_specs, out_specs=out_specs, check_vma=False)
```

```python
import functools
import math

import jax
import jax.numpy as jnp
from jax import lax
from jax.experimental import pallas as pl
from jax.experimental.pallas import tpu as pltpu
from jax.sharding import Mesh, PartitionSpec as P

HEAD_DIM = 128
WINDOW = 4096
N_DOCS = 4
SCALE = 1.0 / 12.0
SCALE2 = math.log2(math.e) / 12.0
NEG = -1e30
FAR = 1 << 30
F32 = jnp.float32
BF16 = jnp.bfloat16
NT = (((1,), (1,)), ((), ()))
NN = (((1,), (0,)), ((), ()))

TOK = 1024
BQ = 512
BK = 512
D_ROWS = 256
W_COLS = 1152

CTX = ("xl", "y", "core")
FSDP = ("z", "xh")


def first_seen(meta, i):
    low = i + 1
    for d in range(N_DOCS):
        low = jnp.maximum(low, jnp.where(i >= meta[d], meta[N_DOCS + d], 0))
    return low


def heads_of(ref, q0):
    rows = pl.ds(q0, BQ)
    return jnp.concatenate([ref[rows, 0:HEAD_DIM], ref[rows, HEAD_DIM : 2 * HEAD_DIM]], 0)


def masked_tile(meta, tile, q0, place):
    i = q0 + lax.broadcasted_iota(jnp.int32, (1, BQ), 1)
    low = first_seen(meta, i) - place
    high = WINDOW + i - place
    row = lax.broadcasted_iota(jnp.int32, (BK, BQ), 0)
    seen = (row >= low) & (row <= high)
    return jnp.concatenate(
        [jnp.where(seen, tile[:, :BQ], NEG), jnp.where(seen, tile[:, BQ:], NEG)], 1
    )


def for_tiles(meta, q0, base, rows, tile):
    low_first = first_seen(meta, q0)
    low_last = first_seen(meta, q0 + BQ - 1)
    begin = jnp.maximum(low_first - base, 0) // BK
    end = jnp.minimum((WINDOW + q0 + BQ - 1 - base) // BK + 1, rows // BK)

    def step(t, carry):
        row = pl.multiple_of((end - 1 - t) * BK, BK)
        place = base + row
        plain = (place >= low_last) & (place + BK - 1 <= WINDOW + q0)

        @pl.when(plain)
        def _():
            tile(row, place, False)

        @pl.when(jnp.logical_not(plain))
        def _():
            tile(row, place, True)

        return carry

    lax.fori_loop(0, end - begin, step, 0)


def for_queries(tok, work):
    def step(t, carry):
        work(pl.multiple_of(t * BQ, BQ), pl.multiple_of(t * 2 * BQ, 2 * BQ))
        return carry

    lax.fori_loop(0, tok // BQ, step, 0)


def forward_tile(meta, q2, q0, k_ref, v_ref, m_ref, acc_ref, row, place, masked):
    k = k_ref[pl.ds(row, BK), :]
    v = v_ref[pl.ds(row, BK), :]
    s = lax.dot_general(k, q2, NT, preferred_element_type=F32)
    if masked:
        s = masked_tile(meta, s, q0, place)
    m_old = m_ref[0:1, :]
    m_new = jnp.maximum(m_old, jnp.max(s, axis=0, keepdims=True))
    p = jnp.exp2((s - m_new) * SCALE2)
    shrink = jnp.exp2((m_old - m_new) * SCALE2)
    v_ones = jnp.concatenate([v.T, jnp.ones((16, BK), BF16)], 0)
    acc_ref[...] = acc_ref[...] * shrink + lax.dot_general(
        v_ones, p.astype(BF16), NN, preferred_element_type=F32
    )
    m_ref[...] = jnp.broadcast_to(m_new, m_ref.shape)


def key_part(ref):
    return ref.at[:, 0:HEAD_DIM]


def value_part(ref):
    return ref.at[:, HEAD_DIM : 2 * HEAD_DIM]


def base_of(meta, base):
    return base if base >= 0 else meta[-base]


def forward_kernel(bases, first, last, meta, q_ref, *refs):
    n = len(bases)
    block_refs, refs = refs[:n], refs[n:]
    if not first:
        (m_in, acc_in), refs = refs[:2], refs[2:]
    one_out, two_out, m_ref, acc_ref = refs

    def work(q0, c0):
        cols = pl.ds(c0, 2 * BQ)
        q2 = heads_of(q_ref, q0)
        m_ref[...] = jnp.full(m_ref.shape, NEG, F32) if first else m_in[:, cols]
        acc_ref[...] = jnp.zeros(acc_ref.shape, F32) if first else acc_in[:, cols]
        for ref, base in zip(block_refs, bases):
            tile = functools.partial(
                forward_tile, meta, q2, q0, key_part(ref), value_part(ref), m_ref, acc_ref
            )
            for_tiles(meta, q0, base_of(meta, base), TOK, tile)
        if last:
            o = (acc_ref[0:HEAD_DIM, :] / acc_ref[HEAD_DIM : HEAD_DIM + 1, :]).T
            one_out[pl.ds(q0, BQ), 0:HEAD_DIM] = o[:BQ].astype(BF16)
            one_out[pl.ds(q0, BQ), HEAD_DIM : 2 * HEAD_DIM] = o[BQ:].astype(BF16)
            two_out[:, cols] = m_ref[...] * SCALE2 + jnp.log2(acc_ref[HEAD_DIM : HEAD_DIM + 8, :])
        else:
            one_out[:, cols] = m_ref[...]
            two_out[:, cols] = acc_ref[...]

    for_queries(TOK, work)


def forward(name, meta, q, blocks, bases, state=(), last=False):
    out = (
        jax.ShapeDtypeStruct((8, 2 * TOK), F32),
        jax.ShapeDtypeStruct((HEAD_DIM + 16, 2 * TOK), F32),
    )
    if last:
        out = (jax.ShapeDtypeStruct((TOK, 2 * HEAD_DIM), BF16), out[0])
    scratch = [pltpu.VMEM((8, 2 * BQ), F32), pltpu.VMEM((HEAD_DIM + 16, 2 * BQ), F32)]
    args = [q] + list(blocks) + list(state)
    kernel = functools.partial(forward_kernel, bases, not state, last)
    return call(kernel, name, len(args), out, scratch, 20)(meta, *args)


def call(kernel, name, n_vmem, out_shape, scratch, vmem_mb, cost=0):
    vmem = pl.BlockSpec(memory_space=pltpu.VMEM)
    return pl.pallas_call(
        kernel,
        out_shape=out_shape,
        in_specs=[pl.BlockSpec(memory_space=pltpu.SMEM)] + [vmem] * n_vmem,
        out_specs=jax.tree.map(lambda _: vmem, out_shape),
        scratch_shapes=scratch,
        compiler_params=pltpu.CompilerParams(vmem_limit_bytes=vmem_mb * 2**20),
        cost_estimate=pl.CostEstimate(flops=cost, bytes_accessed=0, transcendentals=0),
        name=name,
    )


def backward_kernel(bases, first, last, meta, q_ref, do_ref, o_ref, lse_ref, *refs):
    tok = q_ref.shape[0]
    n = len(bases)
    block_refs, refs = refs[:n], refs[n:]
    if not first:
        dqt_in, refs = refs[0], refs[1:]
    part_refs, dq_ref, (dqt, dk, dv) = refs[:n], refs[n], refs[n + 1 :]
    dk[...] = jnp.zeros(dk.shape, F32)
    dv[...] = jnp.zeros(dv.shape, F32)

    def work(q0, c0):
        cols = pl.ds(c0, 2 * BQ)
        q2 = heads_of(q_ref, q0)
        do2 = heads_of(do_ref, q0)
        o2 = heads_of(o_ref, q0)
        delta = jnp.sum((do2.astype(F32) * o2.astype(F32)).T, axis=0, keepdims=True)
        lse = lse_ref[0:1, cols]
        dqt[...] = jnp.zeros(dqt.shape, F32) if first else dqt_in[:, cols]

        def tile(index, row, place, masked):
            ref = block_refs[index]
            k = ref[pl.ds(row, BK), 0:HEAD_DIM]
            v = ref[pl.ds(row, BK), HEAD_DIM : 2 * HEAD_DIM]
            t = lax.dot_general(k, q2, NT, preferred_element_type=F32) * SCALE2 - lse
            if masked:
                t = masked_tile(meta, t, q0, place)
            p = jnp.exp2(t)
            dp = lax.dot_general(v, do2, NT, preferred_element_type=F32)
            ds = (p * (dp - delta)).astype(BF16)
            rows = pl.ds(row, BK)
            dv[index, rows, :] += lax.dot_general(
                p.astype(BF16), do2, NN, preferred_element_type=F32
            )
            dk[index, rows, :] += lax.dot_general(ds, q2, NN, preferred_element_type=F32)
            dqt[...] += lax.dot_general(k.T, ds, NN, preferred_element_type=F32)

        for index, base in enumerate(bases):
            for_tiles(meta, q0, base_of(meta, base), tok, functools.partial(tile, index))
        if last:
            dq = (dqt[...] * SCALE).T
            dq_ref[pl.ds(q0, BQ), 0:HEAD_DIM] = dq[:BQ].astype(BF16)
            dq_ref[pl.ds(q0, BQ), HEAD_DIM : 2 * HEAD_DIM] = dq[BQ:].astype(BF16)
        else:
            dq_ref[:, cols] = dqt[...]

    for_queries(tok, work)
    for index, ref in enumerate(part_refs):
        ref[:, 0:HEAD_DIM] = (dk[index] * SCALE).astype(ref.dtype)
        ref[:, HEAD_DIM : 2 * HEAD_DIM] = dv[index].astype(ref.dtype)


def backward(name, meta, common, blocks, bases, dqt=None, last=False):
    tok = common[0].shape[0]
    n = len(blocks)
    part = jax.ShapeDtypeStruct((tok, 2 * HEAD_DIM), F32 if last else BF16)
    dq = ((tok, 2 * HEAD_DIM), BF16) if last else ((HEAD_DIM, 2 * tok), F32)
    scratch = [
        pltpu.VMEM((HEAD_DIM, 2 * BQ), F32),
        pltpu.VMEM((n, tok, HEAD_DIM), F32),
        pltpu.VMEM((n, tok, HEAD_DIM), F32),
    ]
    args = list(common) + list(blocks) + ([] if dqt is None else [dqt])
    kernel = functools.partial(backward_kernel, bases, dqt is None, last)
    out = (part,) * n + (jax.ShapeDtypeStruct(*dq),)
    cost = 0 if dqt is None or last else 20_000_000_000
    return call(kernel, name, len(args), out, scratch, 30, cost)(meta, *args)


def d_attn_kernel(og_ref, wt_ref, out_ref):
    out_ref[...] = lax.dot_general(
        og_ref[...], wt_ref[...], NN, preferred_element_type=F32
    ).astype(BF16)


def weight_grad_kernel(og_ref, attn_ref, out_ref, attn_t):
    @pl.when(pl.program_id(0) == 0)
    def _():
        attn_t[...] = attn_ref[...].T

    out_ref[...] = lax.dot_general(
        attn_t[...], og_ref[...], NN, preferred_element_type=F32
    ).T.astype(BF16)


def streamed(kernel, name, steps, in_specs, out_spec, out_shape, scratch):
    return pl.pallas_call(
        kernel,
        grid=(steps,),
        out_shape=out_shape,
        in_specs=in_specs,
        out_specs=out_spec,
        scratch_shapes=scratch,
        compiler_params=pltpu.CompilerParams(vmem_limit_bytes=58 * 2**20),
        cost_estimate=pl.CostEstimate(flops=0, bytes_accessed=0, transcendentals=0),
        name=name,
    )


def d_attn_of(out_grad, weight_t):
    tok, width = out_grad.shape
    heads = weight_t.shape[1]
    in_specs = [
        pl.BlockSpec((D_ROWS, width), lambda i: (i, 0)),
        pl.BlockSpec((width, heads), lambda i: (0, 0)),
    ]
    out_spec = pl.BlockSpec((D_ROWS, heads), lambda i: (i, 0))
    out = jax.ShapeDtypeStruct((tok, heads), BF16)
    return streamed(d_attn_kernel, "d_attn", tok // D_ROWS, in_specs, out_spec, out, [])(
        out_grad, weight_t
    )


def weight_grad_of(out_grad, attn):
    tok, width = out_grad.shape
    heads = attn.shape[1]
    in_specs = [
        pl.BlockSpec((tok, W_COLS), lambda i: (0, i)),
        pl.BlockSpec((tok, heads), lambda i: (0, 0)),
    ]
    out_spec = pl.BlockSpec((W_COLS, heads), lambda i: (i, 0))
    out = jax.ShapeDtypeStruct((width, heads), BF16)
    scratch = [pltpu.VMEM((heads, tok), BF16)]
    return streamed(
        weight_grad_kernel, "weight_grad", width // W_COLS, in_specs, out_spec, out, scratch
    )(out_grad, attn)


def out_kernel(n, where, mine_ref, other_ref, *refs):
    attn_refs, refs = refs[:n], refs[n:]
    out_ref = refs[-1]
    cols = out_ref.shape[0]

    def with_weights(w_ref):
        total = None
        for i, a_ref in enumerate(attn_refs):
            w = w_ref[i * cols : (i + 1) * cols, :]
            term = lax.dot_general(w, a_ref[...], NT, preferred_element_type=F32)
            total = term if total is None else total + term
        out_ref[...] = total.astype(out_ref.dtype)

    @pl.when(where[0] == where[1])
    def _():
        with_weights(mine_ref)

    @pl.when(where[0] != where[1])
    def _():
        with_weights(other_ref)


def out_part(name, where, attns, mine, other, dtype):
    args = [mine, other] + list(attns)
    out = jax.ShapeDtypeStruct((mine.shape[0] // len(attns), TOK), dtype)
    kernel = functools.partial(out_kernel, len(attns))
    return call(kernel, name, len(args), out, [], 20)(where, *args)


def ctx_shift(value, steps):
    count = lax.axis_size(CTX)
    leading, last = max(0, -steps), min(count, count - steps)
    return lax.ppermute(value, CTX, [(s, s + steps) for s in range(leading, last)])


def swap(value, axis):
    return lax.ppermute(value, axis, [(0, 1), (1, 0)])


def z_shift(value, steps):
    count = lax.axis_size("z")
    return lax.ppermute(value, "z", [(s, (s + steps) % count) for s in range(count)])


def body(query_rows, key_rows, value_rows, doc_ids, out_weight, out_grad):
    tok = query_rows.shape[0]
    core = lax.axis_index("core")
    even = core == 0
    z = lax.axis_index("z")
    xh = lax.axis_index("xh")
    n_z = lax.axis_size("z")

    weight_t = lax.all_gather(out_weight.T, CTX, axis=0, tiled=True)

    docs = lax.iota(jnp.int32, N_DOCS)
    count = jnp.sum((doc_ids[None, :] == docs[:, None]).astype(jnp.int32), axis=1)
    info = jnp.stack([count // 32, count % 32]).astype(BF16)
    info = jnp.pad(info, ((0, 14), (0, 2 * HEAD_DIM - N_DOCS)))
    kv = jnp.concatenate([jnp.concatenate([key_rows, value_rows], 1), info], 0)
    two = ctx_shift(kv, 2)

    def count_of(block):
        high, low = block[tok, :N_DOCS], block[tok + 1, :N_DOCS]
        return (high.astype(F32) * 32 + low.astype(F32)).astype(jnp.int32)

    local_start = jnp.cumsum(count) - count
    present = count > 0
    odd_base = jnp.where(even, WINDOW - tok, WINDOW - 3 * tok)
    rest_base = jnp.where(even, WINDOW - 3 * tok, WINDOW - tok)

    def meta_of(before):
        return jnp.concatenate(
            [
                jnp.where(present, local_start, FAR),
                jnp.where(present, WINDOW + local_start - before, 0),
                jnp.stack([odd_base, rest_base]).astype(jnp.int32),
            ]
        )

    meta_own = meta_of(jnp.zeros_like(count))
    m, acc = forward("attn_own", meta_own, query_rows, (kv,), (WINDOW,))
    m, two = lax.optimization_barrier((m, two))
    odd = swap(two, "core")
    four = ctx_shift(two, 2)

    between = jnp.where(even | (count_of(two) == 0), 0, tok)
    before_near = count_of(two) + count_of(odd)
    meta_near = meta_of(before_near + between)
    m, acc = forward(
        "attn_near", meta_near, query_rows, (two, odd), (WINDOW - 2 * tok, -8), (m, acc)
    )
    m, four, weight_t = lax.optimization_barrier((m, four, weight_t))
    rest = swap(jnp.where(even, kv, four), "core")
    meta = meta_of(before_near + count_of(four) + count_of(rest))

    weight_z = weight_t.reshape(n_z, 2, -1, weight_t.shape[1])

    def weight_for(steps):
        half = lax.dynamic_slice(
            weight_z, ((z + steps) % n_z, core, 0, 0), (1, 1) + weight_z.shape[2:]
        )
        return half[0, 0]

    fetched = [z_shift(weight_for(s), s) for s in range(1, n_z)]
    attn, lse = forward(
        "attn_far", meta, query_rows, (rest, four), (-9, WINDOW - 4 * tok), (m, acc), last=True
    )
    attns = [attn] + [z_shift(attn, s) for s in range(1, n_z)]

    dw = weight_grad_of(out_grad, attn)
    dw = lax.psum_scatter(dw, ("xl", "y"), scatter_dimension=0, tiled=True)
    dw = dw.reshape(2, -1, dw.shape[1])
    dw_mine = lax.dynamic_index_in_dim(dw, core, 0, keepdims=False)
    dw_other = swap(lax.dynamic_index_in_dim(dw, 1 - core, 0, keepdims=False), "core")
    weight_grad = lax.optimization_barrier(dw_mine.astype(F32) + dw_other.astype(F32)).T

    weight_d, _, fetched = lax.optimization_barrier((weight_t, attn, fetched))
    d_attn = d_attn_of(out_grad, weight_d)
    w_mine = jnp.concatenate([weight_for(0)] + fetched, 0)
    w_other = swap(w_mine, "core")

    common = (query_rows, d_attn, attn, lse)
    rest_part, four_part, dqt = backward(
        "attn_back_far", meta, common, (rest, four), (-9, WINDOW - 4 * tok)
    )
    rest_part, attns = lax.optimization_barrier((rest_part, attns))
    rest_part = [swap(rest_part[:, h : h + HEAD_DIM], "core") for h in (0, HEAD_DIM)]
    rest_part = jnp.concatenate(rest_part, 1).astype(F32)
    four_sum = (four_part.astype(F32) + jnp.where(even, 0.0, rest_part)).astype(BF16)
    out_other = out_part("out_other", jnp.stack([1 - xh, core]), attns, w_mine, w_other, BF16)
    dqt, four_sum, out_other = lax.optimization_barrier((dqt, four_sum, out_other))
    four_sum = ctx_shift(four_sum, -2)
    out_other = swap(out_other, "xh")

    odd_part, two_part, dqt = backward(
        "attn_back_mid", meta, common, (odd, two), (-8, WINDOW - 2 * tok), dqt
    )
    odd_part, four_sum = lax.optimization_barrier((odd_part, four_sum))
    odd_part = [swap(odd_part[:, h : h + HEAD_DIM], "core") for h in (0, HEAD_DIM)]
    odd_part = jnp.concatenate(odd_part, 1).astype(F32)
    two_sum = (two_part.astype(F32) + odd_part + four_sum.astype(F32)).astype(BF16)
    dqt, two_sum = lax.optimization_barrier((dqt, two_sum))
    two_sum = ctx_shift(two_sum, -2)

    own, query_grad = backward("attn_back_own", meta, common, (kv,), (WINDOW,), dqt, last=True)
    layer_out = out_part("out_mine", jnp.stack([xh, core]), attns, w_mine, w_other, F32)
    layer_out = (layer_out + out_other.astype(F32)).astype(BF16).T
    own = own + jnp.where(even, rest_part, 0.0)
    own = (own + two_sum.astype(F32)).astype(BF16)
    return layer_out, query_grad, own[:, :HEAD_DIM], own[:, HEAD_DIM:], weight_grad


def solution(mesh):
    fine = Mesh(mesh.devices.reshape(2, 4, 2, 4, 2), CTX + FSDP)
    in_specs = (
        P(CTX, FSDP),
        P(CTX, FSDP),
        P(CTX, FSDP),
        P(CTX),
        P(FSDP, CTX),
        P(CTX, None),
    )
    out_specs = (
        P(CTX, FSDP),
        P(CTX, FSDP),
        P(CTX, FSDP),
        P(CTX, FSDP),
        P(FSDP, CTX),
    )
    return jax.shard_map(body, mesh=fine, in_specs=in_specs, out_specs=out_specs, check_vma=False)
```

```python
import functools
import math

import jax
import jax.numpy as jnp
from jax import lax
from jax.experimental import pallas as pl
from jax.experimental.pallas import tpu as pltpu
from jax.sharding import Mesh, PartitionSpec as P

HEAD_DIM = 128
WINDOW = 4096
N_DOCS = 4
SCALE = 1.0 / 12.0
SCALE2 = math.log2(math.e) / 12.0
NEG = -1e30
FAR = 1 << 30
F32 = jnp.float32
BF16 = jnp.bfloat16
NT = (((1,), (1,)), ((), ()))
NN = (((1,), (0,)), ((), ()))

TOK = 1024
BQ = 512
BK = 512
D_ROWS = 256
W_COLS = 1152

CTX = ("xl", "y", "core")
FSDP = ("z", "xh")


def first_seen(meta, i):
    low = i + 1
    for d in range(N_DOCS):
        low = jnp.maximum(low, jnp.where(i >= meta[d], meta[N_DOCS + d], 0))
    return low


def heads_of(ref, q0):
    rows = pl.ds(q0, BQ)
    return jnp.concatenate([ref[rows, 0:HEAD_DIM], ref[rows, HEAD_DIM : 2 * HEAD_DIM]], 0)


def masked_tile(meta, tile, q0, place):
    i = q0 + lax.broadcasted_iota(jnp.int32, (1, BQ), 1)
    low = first_seen(meta, i) - place
    high = WINDOW + i - place
    row = lax.broadcasted_iota(jnp.int32, (BK, BQ), 0)
    seen = (row >= low) & (row <= high)
    return jnp.concatenate(
        [jnp.where(seen, tile[:, :BQ], NEG), jnp.where(seen, tile[:, BQ:], NEG)], 1
    )


def for_tiles(meta, q0, base, rows, tile):
    low_first = first_seen(meta, q0)
    low_last = first_seen(meta, q0 + BQ - 1)
    begin = jnp.maximum(low_first - base, 0) // BK
    end = jnp.minimum((WINDOW + q0 + BQ - 1 - base) // BK + 1, rows // BK)

    def step(t, carry):
        row = pl.multiple_of((end - 1 - t) * BK, BK)
        place = base + row
        plain = (place >= low_last) & (place + BK - 1 <= WINDOW + q0)

        @pl.when(plain)
        def _():
            tile(row, place, False)

        @pl.when(jnp.logical_not(plain))
        def _():
            tile(row, place, True)

        return carry

    lax.fori_loop(0, end - begin, step, 0)


def for_queries(tok, work):
    def step(t, carry):
        work(pl.multiple_of(t * BQ, BQ), pl.multiple_of(t * 2 * BQ, 2 * BQ))
        return carry

    lax.fori_loop(0, tok // BQ, step, 0)


def forward_tile(meta, q2, q0, k_ref, v_ref, m_ref, acc_ref, row, place, masked):
    k = k_ref[pl.ds(row, BK), :]
    v = v_ref[pl.ds(row, BK), :]
    s = lax.dot_general(k, q2, NT, preferred_element_type=F32)
    if masked:
        s = masked_tile(meta, s, q0, place)
    m_old = m_ref[0:1, :]
    m_new = jnp.maximum(m_old, jnp.max(s, axis=0, keepdims=True))
    p = jnp.exp2((s - m_new) * SCALE2)
    shrink = jnp.exp2((m_old - m_new) * SCALE2)
    v_ones = jnp.concatenate([v.T, jnp.ones((16, BK), BF16)], 0)
    acc_ref[...] = acc_ref[...] * shrink + lax.dot_general(
        v_ones, p.astype(BF16), NN, preferred_element_type=F32
    )
    m_ref[...] = jnp.broadcast_to(m_new, m_ref.shape)


def key_part(ref):
    return ref.at[:, 0:HEAD_DIM]


def value_part(ref):
    return ref.at[:, HEAD_DIM : 2 * HEAD_DIM]


def base_of(meta, base):
    return base if base >= 0 else meta[-base]


def forward_kernel(bases, first, last, meta, q_ref, *refs):
    n = len(bases)
    block_refs, refs = refs[:n], refs[n:]
    if not first:
        (m_in, acc_in), refs = refs[:2], refs[2:]
    one_out, two_out, m_ref, acc_ref = refs

    def work(q0, c0):
        cols = pl.ds(c0, 2 * BQ)
        q2 = heads_of(q_ref, q0)
        m_ref[...] = jnp.full(m_ref.shape, NEG, F32) if first else m_in[:, cols]
        acc_ref[...] = jnp.zeros(acc_ref.shape, F32) if first else acc_in[:, cols]
        for ref, base in zip(block_refs, bases):
            tile = functools.partial(
                forward_tile, meta, q2, q0, key_part(ref), value_part(ref), m_ref, acc_ref
            )
            for_tiles(meta, q0, base_of(meta, base), TOK, tile)
        if last:
            o = (acc_ref[0:HEAD_DIM, :] / acc_ref[HEAD_DIM : HEAD_DIM + 1, :]).T
            one_out[pl.ds(q0, BQ), 0:HEAD_DIM] = o[:BQ].astype(BF16)
            one_out[pl.ds(q0, BQ), HEAD_DIM : 2 * HEAD_DIM] = o[BQ:].astype(BF16)
            two_out[:, cols] = m_ref[...] * SCALE2 + jnp.log2(acc_ref[HEAD_DIM : HEAD_DIM + 8, :])
        else:
            one_out[:, cols] = m_ref[...]
            two_out[:, cols] = acc_ref[...]

    for_queries(TOK, work)


def forward(name, meta, q, blocks, bases, state=(), last=False):
    out = (
        jax.ShapeDtypeStruct((8, 2 * TOK), F32),
        jax.ShapeDtypeStruct((HEAD_DIM + 16, 2 * TOK), F32),
    )
    if last:
        out = (jax.ShapeDtypeStruct((TOK, 2 * HEAD_DIM), BF16), out[0])
    scratch = [pltpu.VMEM((8, 2 * BQ), F32), pltpu.VMEM((HEAD_DIM + 16, 2 * BQ), F32)]
    args = [q] + list(blocks) + list(state)
    kernel = functools.partial(forward_kernel, bases, not state, last)
    return call(kernel, name, len(args), out, scratch, 20)(meta, *args)


def call(kernel, name, n_vmem, out_shape, scratch, vmem_mb, cost=0):
    vmem = pl.BlockSpec(memory_space=pltpu.VMEM)
    return pl.pallas_call(
        kernel,
        out_shape=out_shape,
        in_specs=[pl.BlockSpec(memory_space=pltpu.SMEM)] + [vmem] * n_vmem,
        out_specs=jax.tree.map(lambda _: vmem, out_shape),
        scratch_shapes=scratch,
        compiler_params=pltpu.CompilerParams(vmem_limit_bytes=vmem_mb * 2**20),
        cost_estimate=pl.CostEstimate(flops=cost, bytes_accessed=0, transcendentals=0),
        name=name,
    )


def backward_kernel(bases, first, last, meta, q_ref, do_ref, o_ref, lse_ref, *refs):
    tok = q_ref.shape[0]
    n = len(bases)
    block_refs, refs = refs[:n], refs[n:]
    if not first:
        dqt_in, refs = refs[0], refs[1:]
    part_refs, dq_ref, (dqt, dk, dv) = refs[:n], refs[n], refs[n + 1 :]
    dk[...] = jnp.zeros(dk.shape, F32)
    dv[...] = jnp.zeros(dv.shape, F32)

    def work(q0, c0):
        cols = pl.ds(c0, 2 * BQ)
        q2 = heads_of(q_ref, q0)
        do2 = heads_of(do_ref, q0)
        o2 = heads_of(o_ref, q0)
        delta = jnp.sum((do2.astype(F32) * o2.astype(F32)).T, axis=0, keepdims=True)
        lse = lse_ref[0:1, cols]
        dqt[...] = jnp.zeros(dqt.shape, F32) if first else dqt_in[:, cols]

        def tile(index, row, place, masked):
            ref = block_refs[index]
            k = ref[pl.ds(row, BK), 0:HEAD_DIM]
            v = ref[pl.ds(row, BK), HEAD_DIM : 2 * HEAD_DIM]
            t = lax.dot_general(k, q2, NT, preferred_element_type=F32) * SCALE2 - lse
            if masked:
                t = masked_tile(meta, t, q0, place)
            p = jnp.exp2(t)
            dp = lax.dot_general(v, do2, NT, preferred_element_type=F32)
            ds = (p * (dp - delta)).astype(BF16)
            rows = pl.ds(row, BK)
            dv[index, rows, :] += lax.dot_general(
                p.astype(BF16), do2, NN, preferred_element_type=F32
            )
            dk[index, rows, :] += lax.dot_general(ds, q2, NN, preferred_element_type=F32)
            dqt[...] += lax.dot_general(k.T, ds, NN, preferred_element_type=F32)

        for index, base in enumerate(bases):
            for_tiles(meta, q0, base_of(meta, base), tok, functools.partial(tile, index))
        if last:
            dq = (dqt[...] * SCALE).T
            dq_ref[pl.ds(q0, BQ), 0:HEAD_DIM] = dq[:BQ].astype(BF16)
            dq_ref[pl.ds(q0, BQ), HEAD_DIM : 2 * HEAD_DIM] = dq[BQ:].astype(BF16)
        else:
            dq_ref[:, cols] = dqt[...]

    for_queries(tok, work)
    for index, ref in enumerate(part_refs):
        ref[:, 0:HEAD_DIM] = (dk[index] * SCALE).astype(ref.dtype)
        ref[:, HEAD_DIM : 2 * HEAD_DIM] = dv[index].astype(ref.dtype)


def backward(name, meta, common, blocks, bases, dqt=None, last=False):
    tok = common[0].shape[0]
    n = len(blocks)
    part = jax.ShapeDtypeStruct((tok, 2 * HEAD_DIM), F32 if last else BF16)
    dq = ((tok, 2 * HEAD_DIM), BF16) if last else ((HEAD_DIM, 2 * tok), F32)
    scratch = [
        pltpu.VMEM((HEAD_DIM, 2 * BQ), F32),
        pltpu.VMEM((n, tok, HEAD_DIM), F32),
        pltpu.VMEM((n, tok, HEAD_DIM), F32),
    ]
    args = list(common) + list(blocks) + ([] if dqt is None else [dqt])
    kernel = functools.partial(backward_kernel, bases, dqt is None, last)
    out = (part,) * n + (jax.ShapeDtypeStruct(*dq),)
    cost = 0 if dqt is None or last else 20_000_000_000
    return call(kernel, name, len(args), out, scratch, 30, cost)(meta, *args)


def d_attn_kernel(og_ref, wt_ref, out_ref):
    out_ref[...] = lax.dot_general(
        og_ref[...], wt_ref[...], NN, preferred_element_type=F32
    ).astype(BF16)


def weight_grad_kernel(og_ref, attn_ref, out_ref, attn_t):
    @pl.when(pl.program_id(0) == 0)
    def _():
        attn_t[...] = attn_ref[...].T

    out_ref[...] = lax.dot_general(
        attn_t[...], og_ref[...], NN, preferred_element_type=F32
    ).T.astype(BF16)


def streamed(kernel, name, steps, in_specs, out_spec, out_shape, scratch):
    return pl.pallas_call(
        kernel,
        grid=(steps,),
        out_shape=out_shape,
        in_specs=in_specs,
        out_specs=out_spec,
        scratch_shapes=scratch,
        compiler_params=pltpu.CompilerParams(vmem_limit_bytes=58 * 2**20),
        cost_estimate=pl.CostEstimate(flops=0, bytes_accessed=0, transcendentals=0),
        name=name,
    )


def d_attn_of(out_grad, weight_t):
    tok, width = out_grad.shape
    heads = weight_t.shape[1]
    in_specs = [
        pl.BlockSpec((D_ROWS, width), lambda i: (i, 0)),
        pl.BlockSpec((width, heads), lambda i: (0, 0)),
    ]
    out_spec = pl.BlockSpec((D_ROWS, heads), lambda i: (i, 0))
    out = jax.ShapeDtypeStruct((tok, heads), BF16)
    return streamed(d_attn_kernel, "d_attn", tok // D_ROWS, in_specs, out_spec, out, [])(
        out_grad, weight_t
    )


def weight_grad_of(out_grad, attn):
    tok, width = out_grad.shape
    heads = attn.shape[1]
    in_specs = [
        pl.BlockSpec((tok, W_COLS), lambda i: (0, i)),
        pl.BlockSpec((tok, heads), lambda i: (0, 0)),
    ]
    out_spec = pl.BlockSpec((W_COLS, heads), lambda i: (i, 0))
    out = jax.ShapeDtypeStruct((width, heads), BF16)
    scratch = [pltpu.VMEM((heads, tok), BF16)]
    return streamed(
        weight_grad_kernel, "weight_grad", width // W_COLS, in_specs, out_spec, out, scratch
    )(out_grad, attn)


def out_kernel(n, where, mine_ref, other_ref, *refs):
    attn_refs, refs = refs[:n], refs[n:]
    out_ref = refs[-1]
    cols = out_ref.shape[0]

    def with_weights(w_ref):
        total = None
        for i, a_ref in enumerate(attn_refs):
            w = w_ref[i * cols : (i + 1) * cols, :]
            term = lax.dot_general(w, a_ref[...], NT, preferred_element_type=F32)
            total = term if total is None else total + term
        out_ref[...] = total.astype(out_ref.dtype)

    @pl.when(where[0] == where[1])
    def _():
        with_weights(mine_ref)

    @pl.when(where[0] != where[1])
    def _():
        with_weights(other_ref)


def out_part(name, where, attns, mine, other, dtype):
    args = [mine, other] + list(attns)
    out = jax.ShapeDtypeStruct((mine.shape[0] // len(attns), TOK), dtype)
    kernel = functools.partial(out_kernel, len(attns))
    return call(kernel, name, len(args), out, [], 20)(where, *args)


def ctx_shift(value, steps):
    count = lax.axis_size(CTX)
    leading, last = max(0, -steps), min(count, count - steps)
    return lax.ppermute(value, CTX, [(s, s + steps) for s in range(leading, last)])


def swap(value, axis):
    return lax.ppermute(value, axis, [(0, 1), (1, 0)])


def z_shift(value, steps):
    count = lax.axis_size("z")
    return lax.ppermute(value, "z", [(s, (s + steps) % count) for s in range(count)])


def body(query_rows, key_rows, value_rows, doc_ids, out_weight, out_grad):
    tok = query_rows.shape[0]
    core = lax.axis_index("core")
    even = core == 0
    z = lax.axis_index("z")
    xh = lax.axis_index("xh")
    n_z = lax.axis_size("z")

    weight_t = lax.all_gather(out_weight.T, CTX, axis=0, tiled=True)

    docs = lax.iota(jnp.int32, N_DOCS)
    count = jnp.sum((doc_ids[None, :] == docs[:, None]).astype(jnp.int32), axis=1)
    info = jnp.stack([count // 32, count % 32]).astype(BF16)
    info = jnp.pad(info, ((0, 14), (0, 2 * HEAD_DIM - N_DOCS)))
    kv = jnp.concatenate([jnp.concatenate([key_rows, value_rows], 1), info], 0)
    two = ctx_shift(kv, 2)
    four = ctx_shift(kv, 4)

    def count_of(block):
        high, low = block[tok, :N_DOCS], block[tok + 1, :N_DOCS]
        return (high.astype(F32) * 32 + low.astype(F32)).astype(jnp.int32)

    local_start = jnp.cumsum(count) - count
    present = count > 0
    odd_base = jnp.where(even, WINDOW - tok, WINDOW - 3 * tok)
    rest_base = jnp.where(even, WINDOW - 3 * tok, WINDOW - tok)

    def meta_of(before):
        return jnp.concatenate(
            [
                jnp.where(present, local_start, FAR),
                jnp.where(present, WINDOW + local_start - before, 0),
                jnp.stack([odd_base, rest_base]).astype(jnp.int32),
            ]
        )

    meta_own = meta_of(jnp.zeros_like(count))
    m, acc = forward("attn_own", meta_own, query_rows, (kv,), (WINDOW,))
    m, two = lax.optimization_barrier((m, two))
    odd = [swap(two[:, h : h + HEAD_DIM], "core") for h in (0, HEAD_DIM)]
    odd = jnp.concatenate(odd, 1)
    m, four = lax.optimization_barrier((m, four))

    between = jnp.where(even | (count_of(two) == 0), 0, tok)
    before_near = count_of(two) + count_of(odd)
    meta_near = meta_of(before_near + between)
    m, acc = forward(
        "attn_near", meta_near, query_rows, (two, odd), (WINDOW - 2 * tok, -8), (m, acc)
    )
    m, weight_t = lax.optimization_barrier((m, weight_t))
    rest = swap(jnp.where(even, kv, four), "core")
    meta = meta_of(before_near + count_of(four) + count_of(rest))

    weight_z = weight_t.reshape(n_z, 2, -1, weight_t.shape[1])

    def weight_for(steps):
        half = lax.dynamic_slice(
            weight_z, ((z + steps) % n_z, core, 0, 0), (1, 1) + weight_z.shape[2:]
        )
        return half[0, 0]

    fetched = [z_shift(weight_for(s), s) for s in range(1, n_z)]
    attn, lse = forward(
        "attn_far", meta, query_rows, (rest, four), (-9, WINDOW - 4 * tok), (m, acc), last=True
    )
    attns = [attn] + [z_shift(attn, s) for s in range(1, n_z)]

    dw = weight_grad_of(out_grad, attn)
    dw = lax.psum_scatter(dw, ("xl", "y"), scatter_dimension=0, tiled=True)
    dw = dw.reshape(2, -1, dw.shape[1])
    dw_mine = lax.dynamic_index_in_dim(dw, core, 0, keepdims=False)
    dw_other = swap(lax.dynamic_index_in_dim(dw, 1 - core, 0, keepdims=False), "core")
    weight_grad = lax.optimization_barrier(dw_mine.astype(F32) + dw_other.astype(F32)).T

    weight_d, _, fetched = lax.optimization_barrier((weight_t, attn, fetched))
    d_attn = d_attn_of(out_grad, weight_d)
    w_mine = jnp.concatenate([weight_for(0)] + fetched, 0)
    w_other = swap(w_mine, "core")

    common = (query_rows, d_attn, attn, lse)
    rest_part, four_part, dqt = backward(
        "attn_back_far", meta, common, (rest, four), (-9, WINDOW - 4 * tok)
    )
    rest_part, attns = lax.optimization_barrier((rest_part, attns))
    rest_part = [swap(rest_part[:, h : h + HEAD_DIM], "core") for h in (0, HEAD_DIM)]
    rest_part = jnp.concatenate(rest_part, 1).astype(F32)
    four_sum = (four_part.astype(F32) + jnp.where(even, 0.0, rest_part)).astype(BF16)
    out_other = out_part("out_other", jnp.stack([1 - xh, core]), attns, w_mine, w_other, BF16)
    dqt, four_sum, out_other = lax.optimization_barrier((dqt, four_sum, out_other))
    four_sum = ctx_shift(four_sum, -2)
    out_other = swap(out_other, "xh")

    odd_part, two_part, dqt = backward(
        "attn_back_mid", meta, common, (odd, two), (-8, WINDOW - 2 * tok), dqt
    )
    odd_part, four_sum = lax.optimization_barrier((odd_part, four_sum))
    odd_part = [swap(odd_part[:, h : h + HEAD_DIM], "core") for h in (0, HEAD_DIM)]
    odd_part = jnp.concatenate(odd_part, 1).astype(F32)
    two_sum = (two_part.astype(F32) + odd_part + four_sum.astype(F32)).astype(BF16)
    dqt, two_sum = lax.optimization_barrier((dqt, two_sum))
    two_sum = ctx_shift(two_sum, -2)

    own, query_grad = backward("attn_back_own", meta, common, (kv,), (WINDOW,), dqt, last=True)
    layer_out = out_part("out_mine", jnp.stack([xh, core]), attns, w_mine, w_other, F32)
    layer_out = (layer_out + out_other.astype(F32)).astype(BF16).T
    own = own + jnp.where(even, rest_part, 0.0)
    own = (own + two_sum.astype(F32)).astype(BF16)
    return layer_out, query_grad, own[:, :HEAD_DIM], own[:, HEAD_DIM:], weight_grad


def solution(mesh):
    fine = Mesh(mesh.devices.reshape(2, 4, 2, 4, 2), CTX + FSDP)
    in_specs = (
        P(CTX, FSDP),
        P(CTX, FSDP),
        P(CTX, FSDP),
        P(CTX),
        P(FSDP, CTX),
        P(CTX, None),
    )
    out_specs = (
        P(CTX, FSDP),
        P(CTX, FSDP),
        P(CTX, FSDP),
        P(CTX, FSDP),
        P(FSDP, CTX),
    )
    return jax.shard_map(body, mesh=fine, in_specs=in_specs, out_specs=out_specs, check_vma=False)
```
